32 devices in a mesh: dp: 4 (over y, x), expert: 8 (over z, core).
Axes of the slice: x: 2, y: 2, z: 4, core: 2. Of those that a mesh axis runs over, the one named last changes fastest.
Arguments:
- tokens: bfloat16 [25216, 768], P(('dp', 'expert')), may hold values from -6 to 6
- attn_qkv: bfloat16 [3, 768, 768], P(None, 'dp'), may hold values from -0.21875 to 0.21875
- attn_out: bfloat16 [768, 768], P('dp'), may hold values from -1.75 to 1.75
- router: bfloat16 [768, 8], P('dp'), may hold values from -0.15625 to 0.15625
- norm_gains: bfloat16 [2, 768], P(None, 'dp'), may hold values from 0.5 to 1.5
- expert_in: bfloat16 [8, 768, 3072], P('expert'), may hold values from -0.21875 to 0.21875
- expert_out: bfloat16 [8, 3072, 768], P('expert'), may hold values from -0.21875 to 0.21875
- routes: int32 [25216, 2], P(('dp', 'expert')), may hold values from 0 to 7, all different within a row; in each aligned block of 394 rows (0 to 393, 394 to 787, ...) at most 160 rows name the same one
- clip_limit: float32 [12], replicated, may hold values from 0.5 to 4
- cotangent: bfloat16 [25216, 768], P(('dp', 'expert')), may hold values from -6 to 6
Outputs:
- layer_out: bfloat16 [25216, 768], P(('dp', 'expert'))
- grad_input: bfloat16 [25216, 768], P(('dp', 'expert'))
- grad_attn_qkv: float32 [3, 768, 768], P(None, 'dp')
- grad_attn_out: float32 [768, 768], P('dp')
- grad_router: float32 [768, 8], P('dp')
- grad_gains: float32 [2, 768], P(None, 'dp')
- grad_expert_in: float32 [8, 768, 3072], P('expert', 'dp')
- grad_expert_out: float32 [8, 3072, 768], P('expert', 'dp')
- head_max: float32 [12], replicated
- clipped_qk: float32 [2, 768, 768], P(None, 'dp')
The draws below stay inside these ranges and needn't reach their ends.
Inputs may be any that keep to these rules, and one draw needn't show every extreme that they name: `routes`: each row names two different experts.
All inputs are finite; a program needn't handle non-finite values.
Results may differ from the reference program's by a relative error of at most 0.02.
Values may be sent and summed in bfloat16 or wider, within the bound.
A program may use at most 192 MiB of HBM per device.

```python
import math
import jax
import jax.numpy as jnp
import numpy as np
from jax import lax

D = 768
HEADS = 12
HEAD_DIM = 64
FF = 3072
SEQ = 197
IMG_DEV = 2
TOK_MB = 394
TOKENS = 25216
EXPERTS = 8
CAP = 128
LOAD_MOST = 160


def block_scale(own_key, shape, shards, smallest, largest):
    def one(dim, blocks):
        heights = jax.random.uniform(jax.random.fold_in(jax.random.fold_in(own_key, 6), dim), (blocks,), jnp.float32, smallest / len(shards), largest / len(shards))
        return jnp.repeat(jnp.exp(heights), shape[dim] // blocks).reshape((-1,) + (1,) * (len(shape) - dim - 1))

    loudness = one(*shards[0])
    for cut in shards[1:]:
        loudness = loudness * one(*cut)
    return loudness


def routed_block(key, own, number, rows, amount, top, most, skew):
    order = jax.random.permutation(key, amount)
    crowded, usual = shares(amount, rows * top, most, skew, True), shares(amount, rows * top, most, skew, False)
    places = jnp.arange(amount)

    def named(lengths, turn):
        used = int((lengths > 0).sum())
        fixed = max(1, used // 4)
        moved = fixed + (places - fixed + turn * (used - fixed)) % max(1, amount - fixed)
        return jnp.zeros((amount,), jnp.int32).at[order[jnp.where(places < fixed, places, moved)]].set(jnp.asarray(lengths, jnp.int32))

    lengths = jnp.where(number % 4 == 0, named(crowded, number // 4), named(usual, number - number // 4 - 1))
    mixed = jax.random.permutation(jax.random.fold_in(own, 3), amount)
    donor, taker = mixed[0:amount // 2 * 2:2], mixed[1:amount // 2 * 2:2]
    room = jnp.minimum(lengths[donor] - 1, most - lengths[taker]) // 2
    room = jnp.where((donor == order[0]) | (taker == order[0]) | (lengths[taker] == 0), 0, jnp.maximum(room, 0))
    moved = jax.random.randint(jax.random.fold_in(own, 4), (amount // 2,), 0, 1 << 20) % (room + 1)
    lengths = lengths.at[donor].add(-moved).at[taker].add(moved)
    items = jnp.searchsorted(jnp.cumsum(lengths), jnp.arange(rows * top), side="right").astype(jnp.int32)
    grid = items.reshape(top, rows).T
    grid = grid[jax.random.permutation(jax.random.fold_in(own, 1), rows)]
    turn = jax.random.randint(jax.random.fold_in(own, 2), (rows, 1), 0, top)
    return jnp.take_along_axis(grid, (jnp.arange(top)[None, :] + turn) % top, axis=1)


def shares(amount, total, limit, slope, full):
    weights = [(1 << 20) // math.isqrt(standing ** slope) + 1 for standing in range(1, amount + 1)]
    largest = limit if full else min(limit, max(-(-total // amount), total * weights[0] // sum(weights)))
    least = 1 if total - largest >= amount - 1 else 0
    given, surplus = [largest] + [least] * (amount - 1), total - largest - least * (amount - 1)
    while surplus > 0:
        movable = [i for i in range(1, amount) if given[i] < largest] or [i for i in range(1, amount) if given[i] < limit]
        whole, remaining = sum([weights[i] for i in movable]), surplus
        for i in movable:
            addition = min(limit - given[i], max(1, remaining * weights[i] // whole), surplus)
            given[i] = given[i] + addition
            surplus = surplus - addition
    return np.array(given)


def normal_values(rng, dims, spread, reach, pieces=(), held_as=jnp.bfloat16):
    drawn = spread * jax.random.normal(rng, dims, jnp.float32)
    if pieces:
        drawn = drawn * block_scale(rng, dims, pieces, -0.22, 0.18)
    return jnp.clip(drawn, -reach, reach).astype(held_as)


def setup_inputs(seed: int = 0) -> dict:
    key_list = jax.random.split(jax.random.key(seed), 11)
    tokens = normal_values(key_list[0], (TOKENS, D), 1.0, 6.0, ((0, 32),))
    attn_qkv = normal_values(key_list[1], (3, D, D), D ** -0.5, 0.21875, ((1, 4),))
    attn_out = normal_values(key_list[2], (D, D), (D // 64) ** -0.5, 1.75, ((0, 4),))
    router = normal_values(key_list[3], (D, EXPERTS), (2 * D) ** -0.5, 0.15625, ((0, 4),))
    norm_gains = jnp.clip(1.0 + 0.1 * jax.random.normal(key_list[4], (2, D), jnp.float32), 0.5, 1.5).astype(jnp.bfloat16)
    expert_in = normal_values(key_list[5], (EXPERTS, D, FF), D ** -0.5, 0.21875, ((0, 8),))
    expert_out = normal_values(key_list[6], (EXPERTS, FF, D), (FF // 4) ** -0.5, 0.21875, ((0, 8),))
    routes_keys = jax.random.split(jax.random.fold_in(key_list[7], 1), TOKENS // TOK_MB)
    routes_turns = jax.random.permutation(jax.random.fold_in(key_list[7], 3), TOKENS // TOK_MB)
    routes = jax.vmap(lambda own, number: routed_block(jax.random.fold_in(key_list[7], 2), own, number, TOK_MB, EXPERTS, 2, LOAD_MOST, 1))(routes_keys, routes_turns).reshape((TOKENS, 2))
    clip_limit = jnp.clip(jnp.exp(jax.random.uniform(key_list[8], (HEADS,), jnp.float32, math.log(0.5), math.log(4.0))), 0.5, 4.0)
    cotangent = normal_values(key_list[9], (TOKENS, D), 1.0, 6.0, ((0, 32),))
    return dict(tokens=tokens, attn_qkv=attn_qkv, attn_out=attn_out, router=router, norm_gains=norm_gains, expert_in=expert_in, expert_out=expert_out, routes=routes, clip_limit=clip_limit, cotangent=cotangent)


epsilon = 1e-06
qk_scale = 0.125
gelu_coeff = 0.7978845608028654
highest = lax.Precision.HIGHEST

@jax.custom_vjp
def low(v):
    return lax.optimization_barrier(v.astype(jnp.bfloat16)).astype(jnp.float32)

@jax.custom_vjp
def low_back(v):
    return v

def low_keep(v):
    return (low(v), None)

def low_pass(kept, grad):
    return (grad,)

def back_keep(v):
    return (v, None)

def back_low(kept, grad):
    return (low(grad),)
low.defvjp(low_keep, low_pass)
low_back.defvjp(back_keep, back_low)

def layer_norm(values_in, gain_row):
    row_mean = lax.optimization_barrier(jnp.mean(values_in, axis=-1, keepdims=True))
    centred = values_in - row_mean
    row_var = lax.optimization_barrier(jnp.mean(centred * centred, axis=-1, keepdims=True))
    return centred * lax.rsqrt(row_var + epsilon) * gain_row

def gelu_tanh(values_in):
    return 0.5 * values_in * (1.0 + jnp.tanh(gelu_coeff * (values_in + 0.044715 * values_in * values_in * values_in)))

def attention_block(token_rows, qkv_weight, out_weight, gain_pair):
    first_norm = low(layer_norm(token_rows, gain_pair[0]))
    projected = low_back(low(jnp.einsum('td,cde->cte', first_norm, qkv_weight, precision=highest)))
    split_heads = projected.reshape(3, IMG_DEV, SEQ, HEADS, HEAD_DIM)
    scores = low_back(jnp.einsum('bqhd,bkhd->bhqk', split_heads[0], split_heads[1], precision=highest) * qk_scale)
    row_top = lax.optimization_barrier(jnp.max(scores, axis=-1, keepdims=True))
    exp_scores = jnp.exp(scores - row_top)
    attn_probs = low(exp_scores / lax.optimization_barrier(jnp.sum(exp_scores, axis=-1, keepdims=True)))
    mixed_heads = low_back(low(jnp.einsum('bhqk,bkhd->bqhd', attn_probs, split_heads[2], precision=highest)))
    attended = low_back(jnp.dot(mixed_heads.reshape(TOK_MB, D), out_weight, precision=highest))
    return (token_rows + attended, lax.optimization_barrier(jnp.max(row_top, axis=(0, 2, 3))))

def expert_block(arrived, weight_in, weight_out):
    pre_act = low_back(jnp.dot(arrived, weight_in, precision=highest))
    hidden = low(gelu_tanh(pre_act))
    return low_back(low(jnp.dot(hidden, weight_out, precision=highest)))

def reference(tokens, attn_qkv, attn_out, router, norm_gains, expert_in, expert_out, routes, clip_limit, cotangent):
    blocks = TOKENS // TOK_MB
    pair_count = 2 * TOK_MB
    flat_expert = routes.reshape(blocks, pair_count).astype(jnp.int32)
    onehot = (flat_expert[:, :, None] == jnp.arange(EXPERTS, dtype=jnp.int32)[None, None, :]).astype(jnp.int32)
    before = jnp.cumsum(onehot, axis=1) - onehot
    slot_index = lax.optimization_barrier(jnp.sum(before * onehot, axis=2)).astype(jnp.int32)
    block_index = jnp.broadcast_to(jnp.arange(blocks, dtype=jnp.int32)[:, None], (blocks, pair_count))
    kept_mask = (slot_index < CAP).reshape(TOKENS, 2).astype(jnp.float32)

    def forward_pass(tokens_full, qkv_full, out_full, router_full, gains_full, in_full, out_expert_full):

        def attend(token_rows):
            return attention_block(token_rows, qkv_full, out_full, gains_full)
        residual, tops = lax.map(jax.checkpoint(attend), tokens_full.reshape(blocks, TOK_MB, D))
        residual = residual.reshape(TOKENS, D)
        second_norm = low(layer_norm(residual, gains_full[1]))
        logits = low_back(jnp.dot(second_norm, router_full, precision=highest))
        chosen = jnp.take_along_axis(logits, routes, axis=1)
        exp_chosen = jnp.exp(chosen - lax.optimization_barrier(jnp.max(chosen, axis=1, keepdims=True)))
        gate_values = exp_chosen / lax.optimization_barrier(jnp.sum(exp_chosen, axis=1, keepdims=True))
        pair_rows = jnp.repeat(second_norm, 2, axis=0).reshape(blocks, pair_count, D)
        buffer = jnp.zeros((blocks, EXPERTS, CAP, D), jnp.float32)
        buffer = buffer.at[block_index, flat_expert, slot_index].set(pair_rows, mode='drop')
        buffer = low_back(buffer)
        per_expert = buffer.transpose(1, 0, 2, 3).reshape(EXPERTS, blocks * CAP, D)

        def run_expert(packed):
            return expert_block(packed[0], packed[1], packed[2])
        produced = lax.map(jax.checkpoint(run_expert), (per_expert, in_full, out_expert_full))
        produced = produced.reshape(EXPERTS, blocks, CAP, D).transpose(1, 0, 2, 3)
        returned = produced.at[block_index, flat_expert, slot_index].get(mode='fill', fill_value=0.0)
        returned = returned.reshape(TOKENS, 2, D)
        combined = lax.optimization_barrier(jnp.sum((gate_values * kept_mask)[:, :, None] * returned, axis=1))
        return (residual + combined, lax.optimization_barrier(jnp.max(tops, axis=0)))
    layer_out, pull_back, head_max = jax.vjp(forward_pass, tokens.astype(jnp.float32), attn_qkv.astype(jnp.float32), attn_out.astype(jnp.float32), router.astype(jnp.float32), norm_gains.astype(jnp.float32), expert_in.astype(jnp.float32), expert_out.astype(jnp.float32), has_aux=True)
    grads = pull_back(cotangent.astype(jnp.float32))
    factor = clip_limit / jnp.maximum(head_max, clip_limit)
    root_scale = jnp.repeat(jnp.sqrt(factor), HEAD_DIM)
    clipped_qk = attn_qkv[:2].astype(jnp.float32) * root_scale[None, None, :]
    return (layer_out.astype(jnp.bfloat16), grads[0].astype(jnp.bfloat16), grads[1], grads[2], grads[3], grads[4], grads[5], grads[6], head_max, clipped_qk)
```

```python
import jax
import jax.numpy as jnp
from jax import lax
from jax.sharding import PartitionSpec as P

D = 768
HEADS = 12
HEAD_DIM = 64
FF = 3072
SEQ = 197
IMG_DEV = 2
MB = 2
TOK_MB = 394


epsilon = 1e-06
qk_scale = 0.125
gelu_coeff = 0.7978845608028654


def norm_parts(values_in):
    row_mean = jnp.mean(values_in, axis=-1, keepdims=True)
    centred = values_in - row_mean
    row_var = jnp.mean(centred * centred, axis=-1, keepdims=True)
    inverse = lax.rsqrt(row_var + epsilon)
    return centred * inverse, inverse


def norm_back(unit, inverse, gain_row, incoming):
    scaled = incoming * gain_row
    mean_one = jnp.mean(scaled, axis=-1, keepdims=True)
    mean_two = jnp.mean(scaled * unit, axis=-1, keepdims=True)
    return (scaled - mean_one - unit * mean_two) * inverse, jnp.sum(incoming * unit, axis=0)


def gelu_both(values_in):
    squared = values_in * values_in
    inner = gelu_coeff * (values_in + 0.044715 * squared * values_in)
    bent = jnp.tanh(inner)
    value = 0.5 * values_in * (1.0 + bent)
    slope = 0.5 * (1.0 + bent) + 0.5 * values_in * (1.0 - bent * bent) * gelu_coeff * (
        1.0 + 3.0 * 0.044715 * squared
    )
    return value, slope


def attention_forward(tokens_wide, gain_row, qkv_weight, out_weight):
    unit, inverse = norm_parts(tokens_wide)
    first_norm = (unit * gain_row).astype(jnp.bfloat16)
    projected = jnp.einsum(
        "td,cde->cte", first_norm, qkv_weight, preferred_element_type=jnp.float32
    ).astype(jnp.bfloat16)
    split_heads = projected.reshape(3, IMG_DEV, SEQ, HEADS, HEAD_DIM)
    scores = (
        jnp.einsum(
            "bqhd,bkhd->bhqk", split_heads[0], split_heads[1], preferred_element_type=jnp.float32
        )
        * qk_scale
    )
    row_top = jnp.max(scores, axis=-1, keepdims=True)
    exp_scores = jnp.exp(scores - row_top)
    attn_probs = exp_scores / jnp.sum(exp_scores, axis=-1, keepdims=True)
    probs_low = attn_probs.astype(jnp.bfloat16)
    mixed_heads = jnp.einsum(
        "bhqk,bkhd->bqhd", probs_low, split_heads[2], preferred_element_type=jnp.float32
    ).astype(jnp.bfloat16)
    mixed_flat = mixed_heads.reshape(TOK_MB, D)
    residual = tokens_wide + jnp.dot(mixed_flat, out_weight, preferred_element_type=jnp.float32)
    head_top = jnp.max(row_top, axis=(0, 2, 3))
    return dict(
        unit=unit,
        inverse=inverse,
        first_norm=first_norm,
        split_heads=split_heads,
        probs=attn_probs,
        probs_low=probs_low,
        mixed=mixed_flat,
        residual=residual,
        head_top=head_top,
    )


def attention_backward(kept, grad_attended, qkv_weight, out_weight):
    split_heads = kept["split_heads"]
    grad_mixed = jnp.einsum(
        "te,de->td", grad_attended, out_weight, preferred_element_type=jnp.float32
    )
    grad_mixed = grad_mixed.astype(jnp.bfloat16).reshape(IMG_DEV, SEQ, HEADS, HEAD_DIM)
    grad_probs = jnp.einsum(
        "bqhd,bkhd->bhqk", grad_mixed, split_heads[2], preferred_element_type=jnp.float32
    )
    grad_values = jnp.einsum(
        "bhqk,bqhd->bkhd", kept["probs_low"], grad_mixed, preferred_element_type=jnp.float32
    )
    row_dot = jnp.sum(kept["probs"] * grad_probs, axis=-1, keepdims=True)
    grad_scores = (kept["probs"] * (grad_probs - row_dot)).astype(jnp.bfloat16)
    grad_queries = (
        jnp.einsum(
            "bhqk,bkhd->bqhd", grad_scores, split_heads[1], preferred_element_type=jnp.float32
        )
        * qk_scale
    )
    grad_keys = (
        jnp.einsum(
            "bhqk,bqhd->bkhd", grad_scores, split_heads[0], preferred_element_type=jnp.float32
        )
        * qk_scale
    )
    grad_proj = [
        part.astype(jnp.bfloat16).reshape(TOK_MB, D)
        for part in (grad_queries, grad_keys, grad_values)
    ]
    grad_first = sum(
        jnp.einsum("te,de->td", grad_proj[c], qkv_weight[c], preferred_element_type=jnp.float32)
        for c in range(3)
    )
    return grad_proj, grad_first


def slot_numbers(route_rows, experts, capacity):
    flat_expert = route_rows.reshape(-1)
    onehot = (flat_expert[:, None] == jnp.arange(experts, dtype=jnp.int32)[None, :]).astype(
        jnp.int32
    )
    before = jnp.cumsum(onehot, axis=0) - onehot
    slot_index = jnp.sum(before * onehot, axis=1)
    kept = slot_index < capacity
    slot_ids = jnp.where(kept, flat_expert * capacity + slot_index, -1)
    return slot_ids.reshape(-1, 2), kept.reshape(-1, 2).astype(jnp.float32)


def exchange(rows):
    return lax.all_to_all(rows, "expert", split_axis=0, concat_axis=0, tiled=True)


def per_device(
    tokens,
    attn_qkv,
    attn_out,
    router,
    norm_gains,
    expert_in,
    expert_out,
    routes,
    clip_limit,
    cotangent,
):
    devices = lax.axis_size("expert")
    experts = devices * expert_in.shape[0]
    capacity = max(8, (TOK_MB * 10 // (4 * experts) + 7) // 8 * 8)
    slots = experts * capacity
    weight_in = expert_in[0]
    weight_out = expert_out[0]
    expert_ids = jnp.arange(experts, dtype=jnp.int32)
    slot_ids_all = jnp.arange(slots, dtype=jnp.int32)

    def block(array, index):
        return lax.slice_in_dim(array, index * TOK_MB, (index + 1) * TOK_MB, axis=0)

    tables, cot_arrived = [], []
    for index in range(MB):
        slot_ids, kept = slot_numbers(block(routes, index), experts, capacity)
        pick = [(slot_ids_all[:, None] == slot_ids[None, :, k]) for k in range(2)]
        token_pick = (pick[0] | pick[1]).astype(jnp.bfloat16)
        tables.append((kept, pick, token_pick))
        packed = jnp.dot(
            token_pick, block(cotangent, index), preferred_element_type=jnp.float32
        ).astype(jnp.bfloat16)
        cot_arrived.append(exchange(packed.reshape(experts, capacity, D)).reshape(slots, D))

    gains = lax.all_gather(norm_gains, "dp", axis=1, tiled=True).astype(jnp.float32)
    qkv_weight = lax.all_gather(attn_qkv, "dp", axis=1, tiled=True)
    out_weight = lax.all_gather(attn_out, "dp", axis=0, tiled=True)
    router_weight = lax.all_gather(router, "dp", axis=0, tiled=True)

    keeps, mids = [], []
    for index in range(MB):
        kept, pick, token_pick = tables[index]
        kept_rows = attention_forward(
            block(tokens, index).astype(jnp.float32), gains[0], qkv_weight, out_weight
        )
        unit_two, inverse_two = norm_parts(kept_rows["residual"])
        second_norm = (unit_two * gains[1]).astype(jnp.bfloat16)
        logits = jnp.dot(second_norm, router_weight, preferred_element_type=jnp.float32)
        named = block(routes, index)[:, :, None] == expert_ids[None, None, :]
        chosen = jnp.sum(jnp.where(named, logits[:, None, :], 0.0), axis=2)
        exp_chosen = jnp.exp(chosen - jnp.max(chosen, axis=1, keepdims=True))
        gate = exp_chosen / jnp.sum(exp_chosen, axis=1, keepdims=True)
        packed = jnp.dot(token_pick, second_norm, preferred_element_type=jnp.float32)
        arrived = exchange(packed.astype(jnp.bfloat16).reshape(experts, capacity, D))
        slot_gate = sum(
            jnp.sum(jnp.where(pick[k], gate[None, :, k], 0.0), axis=1) for k in range(2)
        )
        gate_arrived = exchange(slot_gate.reshape(experts, capacity))
        keeps.append(kept_rows)
        mids.append(
            dict(
                unit=unit_two,
                inverse=inverse_two,
                norm=second_norm,
                gate=gate,
                named=named,
                arrived=arrived.reshape(slots, D),
                gate_arrived=gate_arrived.reshape(slots, 1),
            )
        )

    head_top = jnp.maximum(keeps[0]["head_top"], keeps[1]["head_top"])

    returned, grad_back, gate_back, hiddens, grad_pres, grad_rows_all = [], [], [], [], [], []
    for index in range(MB):
        mid = mids[index]
        cot_wide = cot_arrived[index].astype(jnp.float32)
        pre_act = jnp.dot(mid["arrived"], weight_in, preferred_element_type=jnp.float32)
        value, slope = gelu_both(pre_act)
        hidden = value.astype(jnp.bfloat16)
        grad_rows = (mid["gate_arrived"] * cot_wide).astype(jnp.bfloat16)
        grad_hidden = jnp.einsum(
            "rd,fd->rf", grad_rows, weight_out, preferred_element_type=jnp.float32
        )
        grad_pre = (grad_hidden * slope).astype(jnp.bfloat16)
        grad_sent = jnp.einsum("rf,df->rd", grad_pre, weight_in, preferred_element_type=jnp.float32)
        grad_back.append(
            exchange(grad_sent.astype(jnp.bfloat16).reshape(experts, capacity, D)).reshape(slots, D)
        )
        produced = jnp.dot(hidden, weight_out, preferred_element_type=jnp.float32)
        gate_grad = jnp.sum(produced * cot_wide, axis=1)
        gate_back.append(exchange(gate_grad.reshape(experts, capacity)).reshape(slots))
        returned.append(
            exchange(
                (produced * mid["gate_arrived"])
                .astype(jnp.bfloat16)
                .reshape(experts, capacity, D)
            ).reshape(slots, D)
        )
        hiddens.append(hidden)
        grad_pres.append(grad_pre)
        grad_rows_all.append(grad_rows)

    grad_out = jnp.einsum(
        "rf,rd->fd",
        jnp.concatenate(hiddens, axis=0),
        jnp.concatenate(grad_rows_all, axis=0),
        preferred_element_type=jnp.float32,
    ).astype(jnp.bfloat16)
    grad_out_share = lax.psum_scatter(grad_out[None], "dp", scatter_dimension=1, tiled=True)
    grad_in = jnp.einsum(
        "rd,rf->df",
        jnp.concatenate([mid["arrived"] for mid in mids], axis=0),
        jnp.concatenate(grad_pres, axis=0),
        preferred_element_type=jnp.float32,
    ).astype(jnp.bfloat16)
    grad_in_share = lax.psum_scatter(grad_in[None], "dp", scatter_dimension=1, tiled=True)

    out_blocks, input_grads = [], []
    grad_gain_one, grad_gain_two = 0.0, 0.0
    attended_all, proj_all, logit_all = [], [], []
    for index in range(MB):
        kept, pick, token_pick = tables[index]
        mid, kept_rows = mids[index], keeps[index]
        cot_wide = block(cotangent, index).astype(jnp.float32)
        grad_gate = jnp.stack(
            [
                jnp.sum(jnp.where(pick[k], gate_back[index][:, None], 0.0), axis=0)
                for k in range(2)
            ],
            axis=1,
        )
        grad_chosen = mid["gate"] * (
            grad_gate - jnp.sum(mid["gate"] * grad_gate, axis=1, keepdims=True)
        )
        grad_logits = jnp.sum(
            jnp.where(mid["named"], grad_chosen[:, :, None], 0.0), axis=1
        ).astype(jnp.bfloat16)
        grad_second = jnp.einsum(
            "sp,sd->pd", token_pick, grad_back[index], preferred_element_type=jnp.float32
        ) + jnp.einsum(
            "te,de->td", grad_logits, router_weight, preferred_element_type=jnp.float32
        )
        grad_resid_norm, gain_two = norm_back(mid["unit"], mid["inverse"], gains[1], grad_second)
        grad_resid = cot_wide + grad_resid_norm
        grad_attended = grad_resid.astype(jnp.bfloat16)
        grad_proj, grad_first = attention_backward(
            kept_rows, grad_attended, qkv_weight, out_weight
        )
        grad_tokens, gain_one = norm_back(
            kept_rows["unit"], kept_rows["inverse"], gains[0], grad_first
        )
        input_grads.append((grad_resid + grad_tokens).astype(jnp.bfloat16))
        grad_gain_one += gain_one
        grad_gain_two += gain_two
        attended_all.append(grad_attended)
        proj_all.append(grad_proj)
        logit_all.append(grad_logits)

    def joined(parts):
        return jnp.concatenate(parts, axis=0)

    first_all = joined([kept_rows["first_norm"] for kept_rows in keeps])
    grad_qkv = [
        jnp.einsum(
            "td,te->de",
            first_all,
            joined([grad_proj[c] for grad_proj in proj_all]),
            preferred_element_type=jnp.float32,
        )
        for c in range(3)
    ]
    grad_attn = jnp.einsum(
        "td,te->de",
        joined([kept_rows["mixed"] for kept_rows in keeps]),
        joined(attended_all),
        preferred_element_type=jnp.float32,
    )
    grad_route = jnp.einsum(
        "td,te->de",
        joined([mid["norm"] for mid in mids]),
        joined(logit_all),
        preferred_element_type=jnp.float32,
    )
    small = jnp.concatenate(
        [grad_route, jnp.stack([grad_gain_one, grad_gain_two], axis=1)], axis=1
    )
    packed_grads = jnp.concatenate(grad_qkv + [grad_attn, small], axis=1).astype(jnp.bfloat16)
    share = lax.psum_scatter(packed_grads, "dp", scatter_dimension=0, tiled=True)
    share = lax.psum(share, "expert").astype(jnp.float32)

    for index in range(MB):
        combined = jnp.einsum(
            "sp,sd->pd", tables[index][2], returned[index], preferred_element_type=jnp.float32
        )
        out_blocks.append((keeps[index]["residual"] + combined).astype(jnp.bfloat16))

    head_max = lax.pmax(head_top, ("dp", "expert"))
    factor = clip_limit / jnp.maximum(head_max, clip_limit)
    root_scale = jnp.repeat(jnp.sqrt(factor), HEAD_DIM)
    clipped_qk = attn_qkv[:2].astype(jnp.float32) * root_scale[None, None, :]
    return (
        jnp.concatenate(out_blocks, axis=0),
        jnp.concatenate(input_grads, axis=0),
        jnp.stack([share[:, c * D : (c + 1) * D] for c in range(3)]),
        share[:, 3 * D : 4 * D],
        share[:, 4 * D : 4 * D + experts],
        share[:, 4 * D + experts :].T,
        grad_in_share.astype(jnp.float32),
        grad_out_share.astype(jnp.float32),
        head_max,
        clipped_qk,
    )


def solution(mesh):
    placed = (
        P(("dp", "expert"), None),
        P(None, "dp", None),
        P("dp", None),
        P("dp", None),
        P(None, "dp"),
        P("expert", None, None),
        P("expert", None, None),
        P(("dp", "expert"), None),
        P(),
        P(("dp", "expert"), None),
    )
    return jax.shard_map(
        per_device,
        mesh=mesh,
        in_specs=placed,
        out_specs=(
            P(("dp", "expert"), None),
            P(("dp", "expert"), None),
            P(None, "dp", None),
            P("dp", None),
            P("dp", None),
            P(None, "dp"),
            P("expert", "dp", None),
            P("expert", "dp", None),
            P(),
            P(None, "dp", None),
        ),
        check_vma=False,
    )
```

```python
import functools
import jax
import jax.numpy as jnp
from jax import lax
from jax.experimental import pallas as pl
from jax.experimental.pallas import tpu as pltpu
from jax.sharding import PartitionSpec as P

D = 768
HEADS = 12
HEAD_DIM = 64
FF = 3072
SEQ = 197
IMG_DEV = 2
MB = 2
TOK_MB = 394
SEQ_PAD = 208
TOK_PAD = IMG_DEV * SEQ_PAD
PAIRS = HEADS // 2
CHUNK = 32
COLS = 256

epsilon = 1e-06
qk_scale = 0.125
gelu_coeff = 0.7978845608028654
low = jnp.bfloat16
wide = jnp.float32

NN = (((1,), (0,)), ((), ()))
NT = (((1,), (1,)), ((), ()))
TN = (((0,), (0,)), ((), ()))


def dot(left, right, dims=NN):
    return lax.dot_general(left, right, dims, preferred_element_type=wide)


def rows_of(index, size):
    return pl.ds(pl.multiple_of(index * size, size), size)


def loop(count, body):
    def step(index, carry):
        body(index)
        return carry

    lax.fori_loop(0, count, step, 0)


def norm_parts(values_in):
    row_mean = jnp.sum(values_in, axis=-1, keepdims=True) * (1.0 / D)
    centred = values_in - row_mean
    row_var = jnp.sum(centred * centred, axis=-1, keepdims=True) * (1.0 / D)
    inverse = lax.rsqrt(row_var + epsilon)
    return centred * inverse, inverse


def norm_back(unit, inverse, gain_row, incoming):
    scaled = incoming * gain_row
    mean_one = jnp.sum(scaled, axis=-1, keepdims=True) * (1.0 / D)
    mean_two = jnp.sum(scaled * unit, axis=-1, keepdims=True) * (1.0 / D)
    return (scaled - mean_one - unit * mean_two) * inverse


def fold_rows(values_in):
    return jnp.sum(values_in.reshape(-1, 8, values_in.shape[-1]), axis=0)


def gelu_both(values_in):
    squared = values_in * values_in
    bent = jnp.tanh(values_in * (gelu_coeff + (gelu_coeff * 0.044715) * squared))
    half = 0.5 + 0.5 * bent
    slope = half + half * (1.0 - bent) * values_in * (
        gelu_coeff + (3.0 * 0.044715 * gelu_coeff) * squared
    )
    return values_in * half, slope


def head_mask(half):
    lane = lax.broadcasted_iota(jnp.int32, (1, 2 * HEAD_DIM), 1)
    return (lane // HEAD_DIM) == half


def attention_forward(tok, gains, wqkv, wout, first, qkv, probs, mixed, resid, second, tops):
    def norm_one(index):
        rows = rows_of(index, CHUNK)
        unit, _ = norm_parts(tok[rows, :].astype(wide))
        first[rows, :] = (unit * gains[0:1, :]).astype(low)

    loop(TOK_PAD // CHUNK, norm_one)

    def project(index):
        part, cols = index // (D // COLS), rows_of(index % (D // COLS), COLS)
        qkv[part, :, cols] = dot(first[...], wqkv[part, :, cols]).astype(low)

    loop(3 * (D // COLS), project)

    def attend(index):
        image, pair = index // PAIRS, index % PAIRS
        rows, cols = rows_of(image, SEQ_PAD), rows_of(pair, 2 * HEAD_DIM)
        query, key, value = qkv[0, rows, cols], qkv[1, rows, cols], qkv[2, rows, cols]
        key_id = lax.broadcasted_iota(jnp.int32, (SEQ_PAD, SEQ_PAD), 1)
        row_id = lax.broadcasted_iota(jnp.int32, (SEQ_PAD, 1), 0)
        total = jnp.zeros((SEQ_PAD, 2 * HEAD_DIM), wide)
        for half in range(2):
            mask = head_mask(half)
            scores = dot(jnp.where(mask, query * qk_scale, 0.0).astype(low), key, NT)
            scores = jnp.where(key_id < SEQ, scores, -jnp.inf)
            row_top = jnp.max(scores, axis=-1, keepdims=True)
            exp_scores = jnp.exp(scores - row_top)
            attn = exp_scores * (1.0 / jnp.sum(exp_scores, axis=-1, keepdims=True))
            attn = attn.astype(low)
            probs[2 * index + half] = attn
            total += dot(attn, jnp.where(mask, value, 0.0).astype(low))
            top = jnp.max(jnp.where(row_id < SEQ, row_top, -jnp.inf), axis=0, keepdims=True)
            slot = pl.ds(2 * pair + half, 1)
            tops[slot, :] = jnp.maximum(tops[slot, :], jnp.broadcast_to(top, (1, 128)))
        mixed[rows, cols] = total.astype(low)

    loop(IMG_DEV * PAIRS, attend)

    def add_out(index):
        cols = rows_of(index, COLS)
        resid[:, cols] = tok[:, cols].astype(wide) + dot(mixed[...], wout[:, cols])

    loop(D // COLS, add_out)

    def norm_two(index):
        rows = rows_of(index, CHUNK)
        unit, _ = norm_parts(resid[rows, :])
        second[rows, :] = (unit * gains[1:2, :]).astype(low)

    loop(TOK_PAD // CHUNK, norm_two)


def place_tokens(route, capacity, named, place):
    experts = named.shape[0]
    expert_id = lax.broadcasted_iota(jnp.int32, (experts, TOK_PAD), 0)
    is_named = (route[0:1, :] == expert_id) | (route[1:2, :] == expert_id)
    earlier = lax.broadcasted_iota(jnp.int32, (TOK_PAD, TOK_PAD), 0) < lax.broadcasted_iota(
        jnp.int32, (TOK_PAD, TOK_PAD), 1
    )
    ones = jnp.where(is_named, 1.0, 0.0)
    count = dot(ones.astype(low), jnp.where(earlier, 1.0, 0.0).astype(low))
    named[...] = jnp.where(is_named, count, -1.0)
    slot_id = lax.broadcasted_iota(jnp.int32, (capacity, TOK_PAD), 0).astype(wide)

    def one(expert):
        hit = slot_id == named[pl.ds(expert, 1), :]
        place[rows_of(expert, capacity), :] = jnp.where(hit, 1.0, 0.0).astype(low)

    loop(experts, one)


def split_three(values_in):
    head = values_in.astype(low)
    rest = values_in - head.astype(wide)
    middle = rest.astype(low)
    return [head, middle, (rest - middle.astype(wide)).astype(low)]


def gate_tokens(second, router_t, named, gate):
    logits = dot(router_t[...], second[...], NT)
    is_named = named[...] >= 0.0
    top = jnp.max(jnp.where(is_named, logits, -jnp.inf), axis=0, keepdims=True)
    exp_logits = jnp.where(is_named, jnp.exp(logits - jnp.where(top > -jnp.inf, top, 0.0)), 0.0)
    total = jnp.sum(exp_logits, axis=0, keepdims=True)
    gate[...] = exp_logits / jnp.where(total > 0.0, total, 1.0)


def gate_slots(expert, gate, place, capacity, slot_gate):
    experts = gate.shape[0]
    only = lax.broadcasted_iota(jnp.int32, (experts, 1), 0) == expert
    row = jnp.sum(jnp.where(only, gate[...], 0.0), axis=0, keepdims=True)
    spot = place[rows_of(expert, capacity), :]
    found = sum(
        dot(jnp.broadcast_to(part, (16, TOK_PAD)), spot, NT) for part in split_three(row)
    )
    slot_gate[expert, :, 0:capacity] = found[0:8, :]


def attention_backward(
    tok, gains, wqkv, wout, qkv, probs, resid, grad, attended, proj, scratch, gain_sums, result, cot
):
    def norm_two(index):
        rows = rows_of(index, CHUNK)
        unit, inverse = norm_parts(resid[rows, :])
        incoming = grad[rows, :]
        grad_resid = cot[rows, :].astype(wide) + norm_back(
            unit, inverse, gains[1:2, :], incoming
        )
        gain_sums[1] += fold_rows(incoming * unit)
        grad[rows, :] = grad_resid
        attended[rows, :] = grad_resid.astype(low)

    loop(TOK_PAD // CHUNK, norm_two)

    def through_out(index):
        cols = rows_of(index, COLS)
        scratch[:, cols] = dot(attended[...], wout[cols, :], NT).astype(low)

    loop(D // COLS, through_out)

    def attend(index):
        image, pair = index // PAIRS, index % PAIRS
        rows, cols = rows_of(image, SEQ_PAD), rows_of(pair, 2 * HEAD_DIM)
        query, key, value = qkv[0, rows, cols], qkv[1, rows, cols], qkv[2, rows, cols]
        incoming = scratch[rows, cols]
        shape = (SEQ_PAD, 2 * HEAD_DIM)
        grad_query, grad_key, grad_value = (jnp.zeros(shape, wide) for _ in range(3))
        for half in range(2):
            mask = head_mask(half)
            attn_low = probs[2 * index + half]
            attn = attn_low.astype(wide)
            grad_mixed = jnp.where(mask, incoming, 0.0).astype(low)
            grad_probs = dot(grad_mixed, value, NT)
            grad_value += dot(attn_low, grad_mixed, TN)
            row_dot = jnp.sum(attn * grad_probs, axis=-1, keepdims=True)
            grad_scores = (attn * (grad_probs - row_dot)).astype(low)
            grad_query += dot(grad_scores, jnp.where(mask, key * qk_scale, 0.0).astype(low))
            grad_key += dot(grad_scores, jnp.where(mask, query * qk_scale, 0.0).astype(low), TN)
        proj[0, rows, cols] = grad_query.astype(low)
        proj[1, rows, cols] = grad_key.astype(low)
        proj[2, rows, cols] = grad_value.astype(low)

    loop(IMG_DEV * PAIRS, attend)

    def through_qkv(index):
        cols = rows_of(index, COLS)
        total = dot(proj[0], wqkv[0, cols, :], NT)
        total += dot(proj[1], wqkv[1, cols, :], NT)
        result[:, cols] = total + dot(proj[2], wqkv[2, cols, :], NT)

    loop(D // COLS, through_qkv)

    def norm_one(index):
        rows = rows_of(index, CHUNK)
        unit, inverse = norm_parts(tok[rows, :].astype(wide))
        incoming = result[rows, :]
        gain_sums[0] += fold_rows(incoming * unit)
        grad[rows, :] += norm_back(unit, inverse, gains[0:1, :], incoming)

    loop(TOK_PAD // CHUNK, norm_one)


ANY = pl.BlockSpec(memory_space=pl.ANY)
VMEM = pl.BlockSpec(memory_space=pltpu.VMEM)
MESH = pl.DeviceIdType.MESH
BLOCK_ROWS = 512
MADE_ROWS = 256
BLOCK_FF = 512
GRAD_FF = 256
KIND_COT, KIND_ROW, KIND_GATE, KIND_BACK, KIND_SLOPE, KIND_MADE = range(6)


def wait_bytes(ref, sem):
    pltpu.make_async_copy(ref, ref, sem).wait()


def local_copy(source, target, sem):
    copy = pltpu.make_async_copy(source, target, sem)
    copy.start()
    return copy


def block_kernel(
    n_dp,
    n_ex,
    capacity,
    tok_in,
    cot_in,
    route,
    qkv_in,
    out_in,
    small_in,
    expert_in,
    expert_out,
    layer_out,
    grad_input,
    share,
    share_small,
    share_in,
    share_out,
    tops_out,
    land,
    spill_hidden,
    spill_grad,
    spill_probs,
    spill_qkv,
    spill_rows,
    stage_in,
    stage_out,
    pair_land,
    dp_land,
    part_land,
    half_land,
    wqkv,
    wout,
    small,
    small_t,
    gains,
    resid,
    place,
    named,
    gate,
    send,
    gate_send,
    gate_land,
    slope_send,
    slope_land,
    tops,
    tops_land,
    tops_dp,
    small_pair,
    small_dp,
    small_part,
    small_sum,
    gain_sums,
    gather_send,
    gather_recv,
    ex_send,
    ex_recv,
    rs_send,
    rs_recv,
    red_send,
    red_recv,
    local_sem,
):
    dp, me = lax.axis_index("dp"), lax.axis_index("expert")
    shard = D // n_dp
    slots = n_ex * capacity
    own_rows = rows_of(dp, shard)

    barrier = pltpu.get_barrier_semaphore()

    def greet_ex(step):
        pl.semaphore_signal(
            barrier, inc=1, device_id=(dp, me ^ (step + 1)), device_id_type=MESH
        )

    def greet_dp(step):
        pl.semaphore_signal(
            barrier, inc=1, device_id=(dp ^ (step + 1), me), device_id_type=MESH
        )

    loop(n_ex - 1, greet_ex)
    loop(n_dp - 1, greet_dp)
    pl.semaphore_wait(barrier, n_ex - 1 + n_dp - 1)

    def remote(source, target, send_sem, recv_sem, device):
        pltpu.make_async_remote_copy(
            src_ref=source,
            dst_ref=target,
            send_sem=send_sem,
            recv_sem=recv_sem,
            device_id=device,
            device_id_type=MESH,
        ).start()

    def gather_small(step):
        peer = (dp ^ (step + 1), me)
        remote(small_in, small.at[own_rows, :], gather_send.at[0], gather_recv.at[0], peer)

    def gather_qkv(step):
        peer = (dp ^ (step + 1), me)
        remote(qkv_in, wqkv.at[:, own_rows, :], gather_send.at[1], gather_recv.at[1], peer)

    def gather_out(step):
        peer = (dp ^ (step + 1), me)
        remote(out_in, wout.at[own_rows, :], gather_send.at[2], gather_recv.at[2], peer)

    loop(n_dp - 1, gather_small)
    loop(n_dp - 1, gather_qkv)
    loop(n_dp - 1, gather_out)
    own_copies = [
        local_copy(small_in, small.at[own_rows, :], local_sem.at[0]),
        local_copy(qkv_in, wqkv.at[:, own_rows, :], local_sem.at[1]),
        local_copy(out_in, wout.at[own_rows, :], local_sem.at[2]),
    ]

    def expert_rows(slot, peer):
        return send.at[slot, rows_of(peer, capacity), :]

    def exchange(kind, slot, micro):
        def one(step):
            peer = me ^ (step + 1)
            remote(
                expert_rows(slot, peer),
                land.at[kind, micro, rows_of(me, capacity), :],
                ex_send.at[kind, micro],
                ex_recv.at[kind, micro],
                (dp, peer),
            )

        loop(n_ex - 1, one)

    def keep_own(kind, slot, micro, sem):
        local_copy(
            expert_rows(slot, me), land.at[kind, micro, rows_of(me, capacity), :], sem
        ).wait()

    def exchange_small(source, target, kind, micro):
        def one(step):
            peer = me ^ (step + 1)
            remote(
                source.at[micro, peer],
                target.at[micro, me],
                ex_send.at[kind, micro],
                ex_recv.at[kind, micro],
                (dp, peer),
            )

        loop(n_ex - 1, one)
        target[micro, me] = source[micro, me]

    def await_rows(sems, kind, micro):
        wait_bytes(send.at[0, pl.ds(0, slots - capacity), :], sems.at[kind, micro])

    def await_small(sems, ref, kind, micro):
        wait_bytes(ref.at[micro, pl.ds(0, n_ex - 1)], sems.at[kind, micro])

    def pack(source, slot, micro):
        def one(expert):
            rows = rows_of(expert, capacity)
            send[slot, rows, :] = dot(place[micro, rows, :], source[...]).astype(low)

        loop(n_ex, one)

    def forward(tok, probs, qkv, first, mixed, second, spill_sem):
        def spills(micro):
            tokens = rows_of(micro, TOK_PAD)
            pairs = [
                (probs.at[micro], spill_probs.at[micro]),
                (qkv.at[micro], spill_qkv.at[micro]),
                (first.at[tokens], spill_rows.at[0, tokens]),
                (mixed.at[tokens], spill_rows.at[1, tokens]),
                (second.at[tokens], spill_rows.at[2, tokens]),
            ]
            return [
                pltpu.make_async_copy(source, target, spill_sem.at[micro, index])
                for index, (source, target) in enumerate(pairs)
            ]

        def send_cot(micro):
            local_copy(cot_in.at[micro], tok.at[0], local_sem.at[3]).wait()
            place_tokens(route.at[micro], capacity, named.at[micro], place.at[micro])
            pack(tok.at[0], micro, micro)
            exchange(KIND_COT, micro, micro)
            keep_own(KIND_COT, micro, micro, local_sem.at[3])

        loop(MB, send_cot)
        load = local_copy(tok_in, tok, local_sem.at[3])
        tops[...] = jnp.full(tops.shape, -jnp.inf, wide)
        own_copies[0].wait()
        wait_bytes(small.at[pl.ds(0, D - shard), :], gather_recv.at[0])
        turned = small[...].astype(wide).T
        small_t[...] = turned.astype(low)
        gains[...] = turned[n_ex : n_ex + 8, :]
        load.wait()
        own_copies[1].wait()
        wait_bytes(wqkv.at[:, pl.ds(0, D - shard), :], gather_recv.at[1])
        own_copies[2].wait()
        wait_bytes(wout.at[pl.ds(0, D - shard), :], gather_recv.at[2])

        def one(micro):
            attention_forward(
                tok.at[micro],
                gains,
                wqkv,
                wout,
                first.at[rows_of(micro, TOK_PAD)],
                qkv.at[micro],
                probs.at[micro],
                mixed.at[rows_of(micro, TOK_PAD)],
                resid.at[micro],
                second.at[rows_of(micro, TOK_PAD)],
                tops,
            )
            for copy in spills(micro):
                copy.start()
            rows = second.at[rows_of(micro, TOK_PAD)]
            gate_tokens(rows, small_t.at[pl.ds(0, n_ex)], named.at[micro], gate.at[micro])
            loop(
                n_ex,
                lambda expert: gate_slots(
                    expert, gate.at[micro], place.at[micro], capacity, gate_send.at[micro]
                ),
            )
            exchange_small(gate_send, gate_land, KIND_GATE, micro)
            pack(rows, MB + micro, micro)
            exchange(KIND_ROW, MB + micro, micro)
            keep_own(KIND_ROW, MB + micro, micro, local_sem.at[3])

        loop(MB, one)

        def spread(step):
            peer = me ^ (step + 1)
            remote(tops, tops_land.at[me], red_send.at[0], red_recv.at[0], (dp, peer))

        loop(n_ex - 1, spread)
        tops_land[me] = tops[...]
        for micro in range(MB):
            for copy in spills(micro):
                copy.wait()

    pl.run_scoped(
        forward,
        pltpu.VMEM((MB, TOK_PAD, D), low),
        pltpu.VMEM((MB, IMG_DEV * HEADS, SEQ_PAD, SEQ_PAD), low),
        pltpu.VMEM((MB, 3, TOK_PAD, D), low),
        pltpu.VMEM((MB * TOK_PAD, D), low),
        pltpu.VMEM((MB * TOK_PAD, D), low),
        pltpu.VMEM((MB * TOK_PAD, D), low),
        pltpu.SemaphoreType.DMA((MB, 5)),
    )

    def experts(w_in, w_out, rows_in, cot, grad_rows, rows_t, grad_t, hidden, grad_pre, made, sems):
        load_in = local_copy(expert_in, w_in, sems.at[0])
        load_out = local_copy(expert_out, w_out, sems.at[1])
        eye = lax.broadcasted_iota(jnp.int32, (capacity, capacity), 0) == lax.broadcasted_iota(
            jnp.int32, (capacity, capacity), 1
        )

        def gate_column(micro, source):
            row = gate_land[micro, source, 0:1, 0:capacity]
            return jnp.sum(jnp.where(eye, row, 0.0), axis=1, keepdims=True)

        load_in.wait()
        load_out.wait()

        def one(micro):
            await_rows(ex_recv, KIND_COT, micro)
            await_small(ex_recv, gate_land, KIND_GATE, micro)
            await_rows(ex_recv, KIND_ROW, micro)
            load_rows = local_copy(land.at[KIND_ROW, micro], rows_in, sems.at[0])
            load_cot = local_copy(land.at[KIND_COT, micro], cot, sems.at[1])
            load_rows.wait()
            load_cot.wait()

            def scale(source):
                rows = rows_of(source, capacity)
                wide_cot = cot[rows, :].astype(wide)
                grad_rows[rows, :] = (wide_cot * gate_column(micro, source)).astype(low)

            loop(n_ex, scale)

            def turn(index):
                rows = rows_of(index, 128)
                cols = pl.ds(pl.multiple_of(micro * slots + index * 128, 128), 128)
                rows_t[:, cols] = rows_in[rows, :].T
                grad_t[:, cols] = grad_rows[rows, :].T

            loop(slots // 128, turn)

            @pl.when(micro > 0)
            def _():
                pltpu.make_async_copy(hidden, spill_hidden, sems.at[2]).wait()
                pltpu.make_async_copy(grad_pre, spill_grad, sems.at[3]).wait()

            def through(index):
                cols = rows_of(index // (slots // BLOCK_ROWS), BLOCK_FF)
                rows = rows_of(index % (slots // BLOCK_ROWS), BLOCK_ROWS)
                value, slope = gelu_both(dot(rows_in[rows, :], w_in[:, cols]))
                hidden[rows, cols] = value.astype(low)
                grad_hidden = dot(grad_rows[rows, :], w_out[cols, :], NT)
                grad_pre[rows, cols] = (grad_hidden * slope).astype(low)

            loop((FF // BLOCK_FF) * (slots // BLOCK_ROWS), through)

            @pl.when(micro < MB - 1)
            def _():
                local_copy(hidden, spill_hidden, sems.at[2])
                local_copy(grad_pre, spill_grad, sems.at[3])

            await_rows(ex_send, KIND_COT, micro)

            def back(index):
                rows = rows_of(index, BLOCK_ROWS)
                send[micro, rows, :] = dot(grad_pre[rows, :], w_in[...], NT).astype(low)

            loop(slots // BLOCK_ROWS, back)
            exchange(KIND_BACK, micro, micro)
            await_rows(ex_send, KIND_ROW, micro)

            def forth(index):
                rows = rows_of(index, MADE_ROWS)
                made[...] = dot(hidden[rows, :], w_out[...])
                count = MADE_ROWS // capacity

                def finish(part):
                    source = index * count + part
                    own = rows_of(source, capacity)
                    values = made[rows_of(part, capacity), :]
                    column = jnp.sum(values * cot[own, :].astype(wide), axis=1, keepdims=True)
                    slope_send[micro, source, 0:1, 0:capacity] = jnp.sum(
                        jnp.where(eye, column, 0.0), axis=0, keepdims=True
                    )
                    send[MB + micro, own, :] = (values * gate_column(micro, source)).astype(low)

                loop(count, finish)

            loop(slots // MADE_ROWS, forth)
            exchange_small(slope_send, slope_land, KIND_SLOPE, micro)
            keep_own(KIND_BACK, micro, micro, sems.at[0])

        loop(MB, one)

        def send_made(micro):
            exchange(KIND_MADE, MB + micro, micro)
            keep_own(KIND_MADE, MB + micro, micro, sems.at[0])

        loop(MB, send_made)

        wait_bytes(tops_land.at[pl.ds(0, n_ex - 1)], red_recv.at[0])
        wait_bytes(tops_land.at[pl.ds(0, n_ex - 1)], red_send.at[0])
        tops[...] = jnp.max(tops_land[...], axis=0)

    def expert_phase(w_in, w_out, rows_in, cot, grad_rows, rows_t, grad_t, hidden, grad_pre, made, sems):
        experts(w_in, w_out, rows_in, cot, grad_rows, rows_t, grad_t, hidden, grad_pre, made, sems)
        weight_grads(rows_t, grad_t, hidden, grad_pre)

    def weight_grads(rows_t, grad_t, hidden, grad_pre):
        blocks = FF // GRAD_FF
        half = pl.ds(0, slots)
        other = pl.ds(slots, slots)

        def scoped(kept_hidden, kept_grad, out_in, out_out, load_sems, store_sems):
            def fetch(block, slot):
                cols = rows_of(block, GRAD_FF)
                local_copy(spill_hidden.at[:, cols], kept_hidden.at[slot], load_sems.at[0, slot])
                local_copy(spill_grad.at[:, cols], kept_grad.at[slot], load_sems.at[1, slot])

            def stored(block, slot):
                cols = rows_of(block, GRAD_FF)
                return (
                    pltpu.make_async_copy(
                        out_in.at[slot], stage_in.at[:, cols], store_sems.at[0, slot]
                    ),
                    pltpu.make_async_copy(
                        out_out.at[slot], stage_out.at[:, cols], store_sems.at[1, slot]
                    ),
                )

            def ship(block, slot):
                for copy in stored(block, slot):
                    copy.wait()
                cols = rows_of(block, GRAD_FF)

                def one(step):
                    peer = dp ^ (step + 1)
                    remote(
                        stage_in.at[rows_of(peer, shard), cols],
                        share_in.at[dp, :, cols],
                        rs_send.at[0],
                        rs_recv.at[0],
                        (peer, me),
                    )

                loop(n_dp - 1, one)

            fetch(0, 0)

            def one(block):
                slot = lax.rem(block, 2)

                @pl.when(block + 1 < blocks)
                def _():
                    fetch(block + 1, 1 - slot)

                wait_bytes(kept_hidden.at[slot], load_sems.at[0, slot])
                wait_bytes(kept_grad.at[slot], load_sems.at[1, slot])
                cols = rows_of(block, GRAD_FF)
                out_in[slot] = (
                    dot(rows_t[:, half], kept_grad[slot]) + dot(rows_t[:, other], grad_pre[:, cols])
                ).astype(low)
                out_out[slot] = (
                    dot(grad_t[:, half], kept_hidden[slot]) + dot(grad_t[:, other], hidden[:, cols])
                ).astype(low)
                for copy in stored(block, slot):
                    copy.start()

                @pl.when(block > 0)
                def _():
                    ship(block - 1, 1 - slot)

            loop(blocks, one)
            ship(blocks - 1, (blocks - 1) % 2)

        pl.run_scoped(
            scoped,
            pltpu.VMEM((2, slots, GRAD_FF), low),
            pltpu.VMEM((2, slots, GRAD_FF), low),
            pltpu.VMEM((2, D, GRAD_FF), low),
            pltpu.VMEM((2, D, GRAD_FF), low),
            pltpu.SemaphoreType.DMA((2, 2)),
            pltpu.SemaphoreType.DMA((2, 2)),
        )

    pl.run_scoped(
        expert_phase,
        pltpu.VMEM((D, FF), low),
        pltpu.VMEM((FF, D), low),
        pltpu.VMEM((slots, D), low),
        pltpu.VMEM((slots, D), low),
        pltpu.VMEM((slots, D), low),
        pltpu.VMEM((D, MB * slots), low),
        pltpu.VMEM((D, MB * slots), low),
        pltpu.VMEM((slots, FF), low),
        pltpu.VMEM((slots, FF), low),
        pltpu.VMEM((MADE_ROWS, D), wide),
        pltpu.SemaphoreType.DMA((4,)),
    )

    width = FF // n_dp

    def ship_out(step):
        peer = dp ^ (step + 1)
        remote(
            stage_out.at[:, rows_of(peer, width)],
            share_out.at[dp],
            rs_send.at[1],
            rs_recv.at[1],
            (peer, me),
        )

    loop(n_dp - 1, ship_out)

    def spread_tops(step):
        peer = dp ^ (step + 1)
        remote(tops, tops_dp.at[dp], red_send.at[1], red_recv.at[1], (peer, me))

    loop(n_dp - 1, spread_tops)
    tops_dp[dp] = tops[...]

    parts = n_ex // 2
    part_rows = part_size(n_dp, n_ex)
    core = lax.rem(me, 2)
    z = me // 2

    def backward(
        tok,
        cot,
        probs,
        qkv,
        first,
        mixed,
        second,
        arrived,
        grad,
        attended,
        proj,
        scratch,
        result,
        out,
        grads,
        own,
        half,
        sems,
    ):
        keeps = [
            local_copy(spill_rows.at[index], target, sems.at[7 + index])
            for index, target in enumerate((first, mixed, second))
        ]
        copy_in = local_copy(stage_in.at[own_rows, :], share_in.at[dp], sems.at[5])
        copy_out = local_copy(stage_out.at[:, rows_of(dp, width)], share_out.at[dp], sems.at[6])
        for copy in keeps:
            copy.wait()
        gain_sums[...] = jnp.zeros(gain_sums.shape, wide)
        small_sum[...] = jnp.zeros(small_sum.shape, wide)

        def one(micro):
            tokens = rows_of(micro, TOK_PAD)
            loads = [
                local_copy(tok_in.at[micro], tok, sems.at[0]),
                local_copy(cot_in.at[micro], cot, sems.at[1]),
                local_copy(spill_probs.at[micro], probs, sems.at[2]),
                local_copy(spill_qkv.at[micro], qkv, sems.at[10]),
            ]
            await_small(ex_recv, slope_land, KIND_SLOPE, micro)
            await_rows(ex_recv, KIND_BACK, micro)
            local_copy(land.at[KIND_BACK, micro], arrived, sems.at[3]).wait()

            expert_id = lax.broadcasted_iota(jnp.int32, (n_ex, 1), 0)
            scratch[pl.ds(0, n_ex), 0:TOK_PAD] = jnp.zeros((n_ex, TOK_PAD), wide)

            def slopes(expert):
                row = slope_land[micro, expert, 0:1, 0:capacity]
                spot = place[micro, rows_of(expert, capacity), :]
                found = sum(
                    dot(jnp.broadcast_to(part, (16, capacity)), spot) for part in split_three(row)
                )
                scratch[pl.ds(0, n_ex), 0:TOK_PAD] += jnp.where(
                    expert_id == expert, found[0:1, :], 0.0
                )

            loop(n_ex, slopes)
            gates = gate[micro]
            slope = scratch[pl.ds(0, n_ex), 0:TOK_PAD]
            grad_logits = gates * (slope - jnp.sum(gates * slope, axis=0, keepdims=True))
            grad_logits = grad_logits.astype(low)
            small_sum[pl.ds(0, n_ex), :] += dot(grad_logits, second[tokens, :])
            for block in range(D // COLS):
                cols = pl.ds(block * COLS, COLS)
                grad[:, cols] = dot(place[micro], arrived[:, cols], TN) + dot(
                    grad_logits, small_t[pl.ds(0, n_ex), cols], TN
                )
            for load in loads:
                load.wait()
            attention_backward(
                tok,
                gains,
                wqkv,
                wout,
                qkv,
                probs,
                resid.at[micro],
                grad,
                attended.at[tokens],
                proj.at[:, tokens, :],
                out,
                gain_sums,
                result,
                cot,
            )
            out[...] = grad[...].astype(low)
            local_copy(out, grad_input.at[micro], sems.at[4]).wait()

        loop(MB, one)

        def grad_block(index):
            part, block = index // (D // COLS), index % (D // COLS)
            cols = rows_of(block, COLS)
            value = dot(first[...], proj[part, :, cols], TN).astype(low)
            for owner in range(n_dp):
                grads[part, owner, :, cols] = value[owner * shard : (owner + 1) * shard, :]

        loop(3 * (D // COLS), grad_block)

        def grad_out_block(block):
            cols = rows_of(block, COLS)
            value = dot(mixed[...], attended[:, cols], TN).astype(low)
            for owner in range(n_dp):
                grads[3, owner, :, cols] = value[owner * shard : (owner + 1) * shard, :]

        loop(D // COLS, grad_out_block)
        small_sum[n_ex : n_ex + 1, :] = jnp.sum(gain_sums[0], axis=0, keepdims=True)
        small_sum[n_ex + 1 : n_ex + 2, :] = jnp.sum(gain_sums[1], axis=0, keepdims=True)
        small[...] = small_sum[...].T.astype(low)

        partner = (dp, me ^ 1)
        remote(grads.at[pl.ds(2 - 2 * core, 2)], pair_land, red_send.at[2], red_recv.at[2], partner)
        remote(small, small_pair, red_send.at[3], red_recv.at[3], partner)
        wait_bytes(small_pair, red_recv.at[3])
        wait_bytes(small, red_send.at[3])
        small[...] = (small[...].astype(wide) + small_pair[...].astype(wide)).astype(low)
        wait_bytes(pair_land, red_recv.at[2])

        def add_pair(index):
            part, owner = index // n_dp, index % n_dp
            copy = local_copy(pair_land.at[part, owner], own.at[0], sems.at[0])
            copy.wait()
            mine = grads[2 * core + part, owner].astype(wide)
            half[part, owner] = (mine + own[0].astype(wide)).astype(low)

        loop(2 * n_dp, add_pair)

        def to_owner(step):
            peer = dp ^ (step + 1)
            remote(
                half.at[:, peer], dp_land.at[dp], red_send.at[4], red_recv.at[4], (peer, me)
            )
            remote(
                small.at[rows_of(peer, shard), :],
                small_dp.at[dp],
                red_send.at[5],
                red_recv.at[5],
                (peer, me),
            )

        loop(n_dp - 1, to_owner)
        small_dp[dp] = small[own_rows, :]

        def combine(micro):
            await_rows(ex_recv, KIND_MADE, micro)
            local_copy(land.at[KIND_MADE, micro], arrived, sems.at[3]).wait()
            for block in range(D // COLS):
                cols = pl.ds(block * COLS, COLS)
                out[:, cols] = (
                    resid[micro, :, cols] + dot(place[micro], arrived[:, cols], TN)
                ).astype(low)
            local_copy(out, layer_out.at[micro], sems.at[4]).wait()

        loop(MB, combine)

        wait_bytes(dp_land.at[pl.ds(0, n_dp - 1)], red_recv.at[4])
        wait_bytes(small_dp.at[pl.ds(0, n_dp - 1)], red_recv.at[5])
        for part in range(2):
            result[pl.ds(part * shard, shard), :] = half[part, dp].astype(wide)

            def add_dp(step):
                peer = dp ^ (step + 1)
                local_copy(dp_land.at[peer, part], own.at[0], sems.at[0]).wait()
                result[pl.ds(part * shard, shard), :] += own[0].astype(wide)

            loop(n_dp - 1, add_dp)
        total = parts * part_rows
        if total > 2 * shard:
            scratch[pl.ds(2 * shard, total - 2 * shard), :] = jnp.zeros(
                (total - 2 * shard, D), wide
            )
        scratch[pl.ds(0, 2 * shard), :] = result[pl.ds(0, 2 * shard), :]
        grad_low = arrived
        grad_low[pl.ds(0, total), :] = scratch[pl.ds(0, total), :].astype(low)
        small_owner = jnp.sum(small_dp[...].astype(wide), axis=0).astype(low)
        small_part[me] = small_owner

        def to_part(step):
            peer = z ^ (step + 1)
            remote(
                grad_low.at[rows_of(peer, part_rows), :],
                part_land.at[z],
                red_send.at[6],
                red_recv.at[6],
                (dp, 2 * peer + core),
            )
            remote(
                small_part.at[me],
                small_part.at[me],
                red_send.at[7],
                red_recv.at[7],
                (dp, 2 * peer + core),
            )

        loop(parts - 1, to_part)
        wait_bytes(part_land.at[pl.ds(0, parts - 1)], red_recv.at[6])
        mine = rows_of(z, part_rows)
        result[pl.ds(0, part_rows), :] = grad_low[mine, :].astype(wide)

        def add_part(step):
            peer = z ^ (step + 1)
            local_copy(part_land.at[peer], own.at[0, pl.ds(0, part_rows), :], sems.at[0]).wait()
            result[pl.ds(0, part_rows), :] += own[0, pl.ds(0, part_rows), :].astype(wide)

        loop(parts - 1, add_part)
        out[pl.ds(0, part_rows), :] = result[pl.ds(0, part_rows), :].astype(low)

        def to_all(step):
            peer = z ^ (step + 1)
            remote(
                out.at[pl.ds(0, part_rows), :],
                half_land.at[0, mine, :],
                red_send.at[8],
                red_recv.at[8],
                (dp, 2 * peer + core),
            )

        loop(parts - 1, to_all)
        local_copy(out.at[pl.ds(0, part_rows), :], half_land.at[0, mine, :], sems.at[0]).wait()
        wait_bytes(half_land.at[0, pl.ds(0, (parts - 1) * part_rows), :], red_recv.at[8])
        mine_half = half_land.at[0, pl.ds(0, 2 * shard), :]
        remote(
            mine_half,
            half_land.at[1, pl.ds(0, 2 * shard), :],
            red_send.at[9],
            red_recv.at[9],
            partner,
        )
        local_copy(mine_half, share.at[core], sems.at[0]).wait()
        wait_bytes(small_part.at[pl.ds(0, parts - 1)], red_recv.at[7])
        chosen = jnp.zeros((shard, 128), wide)
        for chip in range(parts):
            chosen += small_part[2 * chip + core].astype(wide)
        share_small[...] = chosen
        wait_bytes(half_land.at[1, pl.ds(0, 2 * shard), :], red_recv.at[9])
        local_copy(
            half_land.at[1, pl.ds(0, 2 * shard), :], share.at[1 - core], sems.at[0]
        ).wait()
        wait_bytes(tops_dp.at[pl.ds(0, n_dp - 1)], red_recv.at[1])
        tops_out[...] = jnp.max(tops_dp[...], axis=0)
        copy_in.wait()
        copy_out.wait()

        wait_bytes(pair_land, red_send.at[2])
        wait_bytes(dp_land.at[pl.ds(0, n_dp - 1)], red_send.at[4])
        wait_bytes(grad_low.at[pl.ds(0, (parts - 1) * part_rows), :], red_send.at[6])
        wait_bytes(grad_low.at[pl.ds(0, (parts - 1) * part_rows), :], red_send.at[8])

    pl.run_scoped(
        backward,
        pltpu.VMEM((TOK_PAD, D), low),
        pltpu.VMEM((TOK_PAD, D), low),
        pltpu.VMEM((IMG_DEV * HEADS, SEQ_PAD, SEQ_PAD), low),
        pltpu.VMEM((3, TOK_PAD, D), low),
        pltpu.VMEM((MB * TOK_PAD, D), low),
        pltpu.VMEM((MB * TOK_PAD, D), low),
        pltpu.VMEM((MB * TOK_PAD, D), low),
        pltpu.VMEM((slots, D), low),
        pltpu.VMEM((TOK_PAD, D), wide),
        pltpu.VMEM((MB * TOK_PAD, D), low),
        pltpu.VMEM((3, MB * TOK_PAD, D), low),
        pltpu.VMEM((TOK_PAD, D), wide),
        pltpu.VMEM((TOK_PAD, D), wide),
        pltpu.VMEM((TOK_PAD, D), low),
        pltpu.VMEM((4, n_dp, shard, D), low),
        pltpu.VMEM((1, shard, D), low),
        pltpu.VMEM((2, n_dp, shard, D), low),
        pltpu.SemaphoreType.DMA((11,)),
    )

    wait_bytes(share_in.at[pl.ds(0, n_dp - 1)], rs_recv.at[0])
    wait_bytes(share_out.at[pl.ds(0, n_dp - 1)], rs_recv.at[1])
    wait_bytes(share_in.at[pl.ds(0, n_dp - 1)], rs_send.at[0])
    wait_bytes(share_out.at[pl.ds(0, n_dp - 1)], rs_send.at[1])
    wait_bytes(small.at[pl.ds(0, D - shard), :], gather_send.at[0])
    wait_bytes(wqkv.at[:, pl.ds(0, D - shard), :], gather_send.at[1])
    wait_bytes(wout.at[pl.ds(0, D - shard), :], gather_send.at[2])
    for micro in range(MB):
        await_rows(ex_send, KIND_BACK, micro)
        await_rows(ex_send, KIND_MADE, micro)
        await_small(ex_send, gate_land, KIND_GATE, micro)
        await_small(ex_send, slope_land, KIND_SLOPE, micro)
    wait_bytes(tops_dp.at[pl.ds(0, n_dp - 1)], red_send.at[1])
    wait_bytes(small_dp.at[pl.ds(0, n_dp - 1)], red_send.at[5])
    wait_bytes(small_part.at[pl.ds(0, parts - 1)], red_send.at[7])
    wait_bytes(half_land.at[1, pl.ds(0, 2 * shard), :], red_send.at[9])


def part_size(n_dp, n_ex):
    shard, parts = D // n_dp, n_ex // 2
    return -(-2 * shard // (parts * 16)) * 16


def run_block(n_dp, n_ex, capacity, operands):
    shard, slots = D // n_dp, n_ex * capacity
    parts, part_rows = n_ex // 2, part_size(n_dp, n_ex)
    total = parts * part_rows
    outs = [
        ((MB, TOK_PAD, D), low),
        ((MB, TOK_PAD, D), low),
        ((2, 2 * shard, D), low),
        ((shard, 128), wide),
        ((n_dp, shard, FF), low),
        ((n_dp, D, FF // n_dp), low),
        ((16, 128), wide),
        ((6, MB, slots, D), low),
        ((slots, FF), low),
        ((slots, FF), low),
        ((MB, IMG_DEV * HEADS, SEQ_PAD, SEQ_PAD), low),
        ((MB, 3, TOK_PAD, D), low),
        ((3, MB * TOK_PAD, D), low),
        ((D, FF), low),
        ((D, FF), low),
        ((2, n_dp, shard, D), low),
        ((n_dp, 2, shard, D), low),
        ((parts, part_rows, D), low),
        ((2, total, D), low),
    ]
    in_vmem = (3, 6)
    return pl.pallas_call(
        functools.partial(block_kernel, n_dp, n_ex, capacity),
        out_shape=[jax.ShapeDtypeStruct(*one) for one in outs],
        in_specs=[ANY, ANY, VMEM, ANY, ANY, ANY, ANY, ANY],
        out_specs=[VMEM if index in in_vmem else ANY for index in range(len(outs))],
        scratch_shapes=[
            pltpu.VMEM((3, D, D), low),
            pltpu.VMEM((D, D), low),
            pltpu.VMEM((D, 128), low),
            pltpu.VMEM((128, D), low),
            pltpu.VMEM((8, D), wide),
            pltpu.VMEM((MB, TOK_PAD, D), wide),
            pltpu.VMEM((MB, slots, TOK_PAD), low),
            pltpu.VMEM((MB, n_ex, TOK_PAD), wide),
            pltpu.VMEM((MB, n_ex, TOK_PAD), wide),
            pltpu.VMEM((2 * MB, slots, D), low),
            pltpu.VMEM((MB, n_ex, 8, 128), wide),
            pltpu.VMEM((MB, n_ex, 8, 128), wide),
            pltpu.VMEM((MB, n_ex, 8, 128), wide),
            pltpu.VMEM((MB, n_ex, 8, 128), wide),
            pltpu.VMEM((16, 128), wide),
            pltpu.VMEM((n_ex, 16, 128), wide),
            pltpu.VMEM((n_dp, 16, 128), wide),
            pltpu.VMEM((D, 128), low),
            pltpu.VMEM((n_dp, shard, 128), low),
            pltpu.VMEM((n_ex, shard, 128), low),
            pltpu.VMEM((128, D), wide),
            pltpu.VMEM((2, 8, D), wide),
            pltpu.SemaphoreType.DMA((3,)),
            pltpu.SemaphoreType.DMA((3,)),
            pltpu.SemaphoreType.DMA((6, MB)),
            pltpu.SemaphoreType.DMA((6, MB)),
            pltpu.SemaphoreType.DMA((2,)),
            pltpu.SemaphoreType.DMA((2,)),
            pltpu.SemaphoreType.DMA((10,)),
            pltpu.SemaphoreType.DMA((10,)),
            pltpu.SemaphoreType.DMA((4,)),
        ],
        compiler_params=pltpu.CompilerParams(
            collective_id=0, has_side_effects=True, vmem_limit_bytes=60 * 2**20
        ),
        name="encoder_block",
    )(*operands)


def padded(rows, fill=0):
    images = rows.reshape(MB, IMG_DEV, SEQ, rows.shape[-1])
    images = jnp.pad(
        images, ((0, 0), (0, 0), (0, SEQ_PAD - SEQ), (0, 0)), constant_values=fill
    )
    return images.reshape(MB, TOK_PAD, rows.shape[-1])


def unpadded(rows):
    images = rows.reshape(MB * IMG_DEV, SEQ_PAD, D)[:, :SEQ]
    return images.reshape(MB * TOK_MB, D)


def per_device(
    tokens,
    attn_qkv,
    attn_out,
    router,
    norm_gains,
    expert_in,
    expert_out,
    routes,
    clip_limit,
    cotangent,
):
    n_dp, n_ex = lax.axis_size("dp"), lax.axis_size("expert")
    capacity = max(8, (TOK_MB * 10 // (4 * n_ex) + 7) // 8 * 8)
    shard = D // n_dp
    small = jnp.concatenate(
        [router, norm_gains.T, jnp.zeros((shard, 128 - n_ex - 2), low)], axis=1
    )
    results = run_block(
        n_dp,
        n_ex,
        capacity,
        (
            padded(tokens),
            padded(cotangent),
            jnp.swapaxes(padded(routes, -1), 1, 2),
            attn_qkv,
            attn_out,
            small,
            expert_in[0],
            expert_out[0],
        ),
    )
    layer_out, grad_input, share, share_small, share_in, share_out, tops = results[:7]
    share = share.reshape(4, shard, D).astype(wide)
    head_max = tops[:HEADS, 0]
    factor = clip_limit / jnp.maximum(head_max, clip_limit)
    root_scale = jnp.repeat(jnp.sqrt(factor), HEAD_DIM)
    clipped_qk = attn_qkv[:2].astype(wide) * root_scale[None, None, :]
    return (
        unpadded(layer_out),
        unpadded(grad_input),
        share[:3],
        share[3],
        share_small[:, :n_ex],
        share_small[:, n_ex : n_ex + 2].T,
        jnp.sum(share_in.astype(wide), axis=0)[None],
        jnp.sum(share_out.astype(wide), axis=0).T[None],
        head_max,
        clipped_qk,
    )


def solution(mesh):
    placed = (
        P(("dp", "expert"), None),
        P(None, "dp", None),
        P("dp", None),
        P("dp", None),
        P(None, "dp"),
        P("expert", None, None),
        P("expert", None, None),
        P(("dp", "expert"), None),
        P(),
        P(("dp", "expert"), None),
    )
    return jax.shard_map(
        per_device,
        mesh=mesh,
        in_specs=placed,
        out_specs=(
            P(("dp", "expert"), None),
            P(("dp", "expert"), None),
            P(None, "dp", None),
            P("dp", None),
            P("dp", None),
            P(None, "dp"),
            P("expert", "dp", None),
            P("expert", "dp", None),
            P(),
            P(None, "dp", None),
        ),
        check_vma=False,
    )
```

```python
import functools
import jax
import jax.numpy as jnp
from jax import lax
from jax.experimental import pallas as pl
from jax.experimental.pallas import tpu as pltpu
from jax.sharding import PartitionSpec as P

D = 768
HEADS = 12
HEAD_DIM = 64
FF = 3072
SEQ = 197
IMG_DEV = 2
MB = 2
TOK_MB = 394
SEQ_PAD = 208
TOK_PAD = IMG_DEV * SEQ_PAD
PAIRS = HEADS // 2
UNROLL = 6
COLS = 256

epsilon = 1e-06
qk_scale = 0.125
gelu_coeff = 0.7978845608028654
low = jnp.bfloat16
wide = jnp.float32

NN = (((1,), (0,)), ((), ()))
NT = (((1,), (1,)), ((), ()))
TN = (((0,), (0,)), ((), ()))


def dot(left, right, dims=NN):
    return lax.dot_general(left, right, dims, preferred_element_type=wide)


def rows_of(index, size):
    return pl.ds(pl.multiple_of(index * size, size), size)


def loop(count, body, unroll=1):
    def step(index, carry):
        body(index)
        return carry

    lax.fori_loop(0, count, step, 0, unroll=unroll)


def norm_parts(values_in):
    row_mean = jnp.sum(values_in, axis=-1, keepdims=True) * (1.0 / D)
    centred = values_in - row_mean
    row_var = jnp.sum(centred * centred, axis=-1, keepdims=True) * (1.0 / D)
    inverse = lax.rsqrt(row_var + epsilon)
    return centred * inverse, inverse


def norm_back(unit, inverse, gain_row, incoming):
    scaled = incoming * gain_row
    mean_one = jnp.sum(scaled, axis=-1, keepdims=True) * (1.0 / D)
    mean_two = jnp.sum(scaled * unit, axis=-1, keepdims=True) * (1.0 / D)
    return (scaled - mean_one - unit * mean_two) * inverse


def fold_rows(values_in):
    return jnp.sum(values_in.reshape(-1, 8, values_in.shape[-1]), axis=0)


def gelu_both(values_in):
    squared = values_in * values_in
    bent = jnp.tanh(values_in * (gelu_coeff + (gelu_coeff * 0.044715) * squared))
    half = 0.5 + 0.5 * bent
    slope = half + half * (1.0 - bent) * values_in * (
        gelu_coeff + (3.0 * 0.044715 * gelu_coeff) * squared
    )
    return values_in * half, slope


def head_mask(half):
    lane = lax.broadcasted_iota(jnp.int32, (1, 2 * HEAD_DIM), 1)
    return (lane // HEAD_DIM) == half


def attention_forward(
    tok, gains, wqkv, wout, first, qkv, probs, mixed, resid, second, tops, after_qkv, before_out
):
    def norm_one(index):
        rows = rows_of(index, TOK_PAD)
        unit, _ = norm_parts(tok[rows, :].astype(wide))
        first[rows, :] = (unit * gains[0:1, :]).astype(low)

    loop(1, norm_one)

    def project(index):
        part, cols = index // (D // COLS), rows_of(index % (D // COLS), COLS)
        qkv[part, :, cols] = dot(first[...], wqkv[part, :, cols]).astype(low)

    loop(3 * (D // COLS), project)
    after_qkv()

    def attend(index):
        image, pair = index // PAIRS, index % PAIRS
        rows, cols = rows_of(image, SEQ_PAD), rows_of(pair, 2 * HEAD_DIM)
        query, key, value = qkv[0, rows, cols], qkv[1, rows, cols], qkv[2, rows, cols]
        key_id = lax.broadcasted_iota(jnp.int32, (SEQ_PAD, SEQ_PAD), 1)
        row_id = lax.broadcasted_iota(jnp.int32, (SEQ_PAD, 1), 0)
        total = jnp.zeros((SEQ_PAD, 2 * HEAD_DIM), wide)
        for half in range(2):
            mask = head_mask(half)
            scores = dot(jnp.where(mask, query * qk_scale, 0.0).astype(low), key, NT)
            scores = jnp.where(key_id < SEQ, scores, -jnp.inf)
            row_top = jnp.max(scores, axis=-1, keepdims=True)
            exp_scores = jnp.exp(scores - row_top)
            attn = exp_scores * (1.0 / jnp.sum(exp_scores, axis=-1, keepdims=True))
            attn = attn.astype(low)
            probs[2 * index + half] = attn
            total += dot(attn, jnp.where(mask, value, 0.0).astype(low))
            top = jnp.max(jnp.where(row_id < SEQ, row_top, -jnp.inf), axis=0, keepdims=True)
            slot = pl.ds(2 * pair + half, 1)
            tops[slot, :] = jnp.maximum(tops[slot, :], jnp.broadcast_to(top, (1, 128)))
        mixed[rows, cols] = total.astype(low)

    loop(IMG_DEV * PAIRS, attend, UNROLL)
    before_out()

    def add_out(index):
        cols = rows_of(index, COLS)
        resid[:, cols] = tok[:, cols].astype(wide) + dot(mixed[...], wout[:, cols])

    loop(D // COLS, add_out)

    def norm_two(index):
        rows = rows_of(index, TOK_PAD)
        unit, _ = norm_parts(resid[rows, :])
        second[rows, :] = (unit * gains[1:2, :]).astype(low)

    loop(1, norm_two)


def spread_rows(raw, buffer, padded):
    count = raw.shape[0]
    buffer[pl.ds(0, count), :] = raw[...].astype(wide)
    buffer[pl.ds(count, SEQ_PAD - SEQ + 1), :] = jnp.zeros((SEQ_PAD - SEQ + 1, D), wide)
    inside = lax.broadcasted_iota(jnp.int32, (SEQ_PAD, 1), 0) < SEQ
    for image in range(MB * IMG_DEV):
        rows = buffer[pl.ds(image * SEQ, SEQ_PAD), :]
        spot = pl.ds((image % IMG_DEV) * SEQ_PAD, SEQ_PAD)
        padded[image // IMG_DEV, spot, :] = jnp.where(inside, rows, 0.0).astype(low)


def compact_rows(padded, buffer, target):
    for image in range(MB * IMG_DEV):
        spot = pl.ds((image % IMG_DEV) * SEQ_PAD, SEQ_PAD)
        buffer[pl.ds(image * SEQ, SEQ_PAD), :] = padded[image // IMG_DEV, spot, :]
    target[...] = buffer[pl.ds(0, target.shape[0]), :].astype(low)


def place_tokens(route, capacity, named, place, first, count):
    experts = named.shape[0]
    expert_id = lax.broadcasted_iota(jnp.int32, (experts, TOK_PAD), 0)
    is_named = (route[0:1, :] == expert_id) | (route[1:2, :] == expert_id)
    earlier = lax.broadcasted_iota(jnp.int32, (TOK_PAD, TOK_PAD), 0) < lax.broadcasted_iota(
        jnp.int32, (TOK_PAD, TOK_PAD), 1
    )
    ones = jnp.where(is_named, 1.0, 0.0)
    before = dot(ones.astype(low), jnp.where(earlier, 1.0, 0.0).astype(low))
    named[...] = jnp.where(is_named, before, -1.0)
    slot_id = lax.broadcasted_iota(jnp.int32, (capacity, TOK_PAD), 0).astype(wide)

    def one(index):
        hit = slot_id == named[pl.ds(first + index, 1), :]
        place[rows_of(index, capacity), :] = jnp.where(hit, 1.0, 0.0).astype(low)

    loop(count, one)


def split_three(values_in):
    head = values_in.astype(low)
    rest = values_in - head.astype(wide)
    middle = rest.astype(low)
    return [head, middle, (rest - middle.astype(wide)).astype(low)]


def gate_tokens(second, router_t, named, gate):
    logits = dot(router_t[...], second[...], NT)
    is_named = named[...] >= 0.0
    top = jnp.max(jnp.where(is_named, logits, -jnp.inf), axis=0, keepdims=True)
    exp_logits = jnp.where(is_named, jnp.exp(logits - jnp.where(top > -jnp.inf, top, 0.0)), 0.0)
    total = jnp.sum(exp_logits, axis=0, keepdims=True)
    gate[...] = exp_logits / jnp.where(total > 0.0, total, 1.0)


def own_columns(experts, capacity):
    shape = (experts, experts * capacity)
    column = lax.broadcasted_iota(jnp.int32, shape, 1) // capacity
    return column == lax.broadcasted_iota(jnp.int32, shape, 0)


def exact_dot(left, right, dims):
    count = left.shape[0]
    found = dot(jnp.concatenate(split_three(left), axis=0), right, dims)
    return found[0:count] + found[count : 2 * count] + found[2 * count : 3 * count]


def gate_slots(gate, place, capacity, slot_gate):
    experts = gate.shape[0]
    found = exact_dot(gate[...], place[...], NT)
    row = jnp.sum(jnp.where(own_columns(experts, capacity), found, 0.0), axis=0, keepdims=True)
    for expert in range(experts):
        slot_gate[expert, 0:1, 0:capacity] = row[:, expert * capacity : (expert + 1) * capacity]


def backward_scores(
    gains, wout, qkv, probs, resid, grad, attended, proj, scratch, gain_sums, cot, after_norm
):
    def norm_two(index):
        rows = rows_of(index, TOK_PAD)
        unit, inverse = norm_parts(resid[rows, :])
        incoming = grad[rows, :]
        grad_resid = cot[rows, :].astype(wide) + norm_back(
            unit, inverse, gains[1:2, :], incoming
        )
        gain_sums[1] += fold_rows(incoming * unit)
        grad[rows, :] = grad_resid
        attended[rows, :] = grad_resid.astype(low)

    loop(1, norm_two)
    after_norm()

    def through_out(index):
        cols = rows_of(index, COLS)
        scratch[:, cols] = dot(attended[...], wout[cols, :], NT).astype(low)

    loop(D // COLS, through_out)

    def attend(index):
        image, pair = index // PAIRS, index % PAIRS
        rows, cols = rows_of(image, SEQ_PAD), rows_of(pair, 2 * HEAD_DIM)
        query, key, value = qkv[0, rows, cols], qkv[1, rows, cols], qkv[2, rows, cols]
        incoming = scratch[rows, cols]
        shape = (SEQ_PAD, 2 * HEAD_DIM)
        grad_query, grad_key, grad_value = (jnp.zeros(shape, wide) for _ in range(3))
        for half in range(2):
            mask = head_mask(half)
            attn_low = probs[2 * index + half]
            attn = attn_low.astype(wide)
            grad_mixed = jnp.where(mask, incoming, 0.0).astype(low)
            grad_probs = dot(grad_mixed, value, NT)
            grad_value += dot(attn_low, grad_mixed, TN)
            row_dot = jnp.sum(attn * grad_probs, axis=-1, keepdims=True)
            grad_scores = (attn * (grad_probs - row_dot)).astype(low)
            grad_query += dot(grad_scores, jnp.where(mask, key * qk_scale, 0.0).astype(low))
            grad_key += dot(grad_scores, jnp.where(mask, query * qk_scale, 0.0).astype(low), TN)
        proj[0, rows, cols] = grad_query.astype(low)
        proj[1, rows, cols] = grad_key.astype(low)
        proj[2, rows, cols] = grad_value.astype(low)

    loop(IMG_DEV * PAIRS, attend, UNROLL)


def backward_input(tok, gains, wqkv, grad, proj, gain_sums, result):
    def through_qkv(index):
        cols = rows_of(index, COLS)
        total = dot(proj[0], wqkv[0, cols, :], NT)
        total += dot(proj[1], wqkv[1, cols, :], NT)
        result[:, cols] = total + dot(proj[2], wqkv[2, cols, :], NT)

    loop(D // COLS, through_qkv)

    def norm_one(index):
        rows = rows_of(index, TOK_PAD)
        unit, inverse = norm_parts(tok[rows, :].astype(wide))
        incoming = result[rows, :]
        gain_sums[0] += fold_rows(incoming * unit)
        grad[rows, :] += norm_back(unit, inverse, gains[0:1, :], incoming)

    loop(1, norm_one)


ANY = pl.BlockSpec(memory_space=pl.ANY)
VMEM = pl.BlockSpec(memory_space=pltpu.VMEM)
MESH = pl.DeviceIdType.MESH
BLOCK_ROWS = 512
MADE_ROWS = 256
BLOCK_FF = 512
GRAD_FF = 256
KIND_COT, KIND_ROW, KIND_BACK, KIND_MADE, KIND_GATE, KIND_SLOPE = range(6)


def wait_bytes(ref, sem):
    pltpu.make_async_copy(ref, ref, sem).wait()


def local_copy(source, target, sem):
    copy = pltpu.make_async_copy(source, target, sem)
    copy.start()
    return copy


def block_kernel(
    n_dp,
    n_ex,
    capacity,
    tok_in,
    cot_in,
    route_in,
    qkv_in,
    out_in,
    router_in,
    gains_in,
    expert_in,
    expert_out,
    layer_out,
    grad_input,
    share,
    share_small,
    share_in,
    share_out,
    tops_out,
    land,
    spill_hidden,
    spill_grad,
    spill_probs,
    spill_qkv,
    spill_rows,
    spill_tok,
    spill_cot,
    spill_resid,
    land_qkv,
    land_out,
    hub_rows,
    hub_blocks,
    far_land,
    stage_in,
    stage_out,
    pair_land,
    dp_land,
    part_land,
    route,
    route_far,
    small_own,
    small_land,
    small_t,
    router_low,
    gains,
    second,
    place,
    place_far,
    named,
    named_far,
    gate,
    send,
    hub_buf,
    hub_sums,
    gate_send,
    gate_land,
    slope_send,
    slope_land,
    tops,
    tops_land,
    tops_dp,
    small_sum,
    small_pair,
    small_cut,
    small_dp,
    small_part,
    gain_sums,
    gather_send,
    gather_recv,
    share_send,
    share_sem,
    ex_send,
    ex_recv,
    far_send,
    far_recv,
    full_send,
    full_recv,
    hub_recv,
    sum_send,
    sum_recv,
    route_recv,
    own_near,
    own_far,
    own_hub,
    hub_sem,
    rs_send,
    rs_recv,
    red_send,
    red_recv,
    pair_send,
    pair_recv,
    own_send,
    own_recv,
    local_sem,
):
    dp, me = lax.axis_index("dp"), lax.axis_index("expert")
    shard = D // n_dp
    slots = n_ex * capacity
    own_rows = rows_of(dp, shard)

    barrier = pltpu.get_barrier_semaphore()

    def greet_ex(step):
        pl.semaphore_signal(
            barrier, inc=1, device_id=(dp, me ^ (step + 1)), device_id_type=MESH
        )

    def greet_dp(step):
        pl.semaphore_signal(
            barrier, inc=1, device_id=(dp ^ (step + 1), me), device_id_type=MESH
        )

    loop(n_ex - 1, greet_ex)
    loop(n_dp - 1, greet_dp)
    pl.semaphore_wait(barrier, n_ex - 1 + n_dp - 1)

    def remote(source, target, send_sem, recv_sem, device):
        pltpu.make_async_remote_copy(
            src_ref=source,
            dst_ref=target,
            send_sem=send_sem,
            recv_sem=recv_sem,
            device_id=device,
            device_id_type=MESH,
        ).start()

    small_own[...] = jnp.zeros(small_own.shape, wide)
    small_own[0:n_ex, 0:shard] = router_in[...].astype(wide)
    small_own[n_ex : n_ex + 2, 0:shard] = gains_in[...].astype(wide)

    def gather_small(step):
        peer = (dp ^ (step + 1), me)
        remote(small_own, small_land.at[dp], gather_send.at[0], gather_recv.at[0], peer)

    core = lax.rem(me, 2)
    partner = (dp, me ^ 1)
    half_shard = shard // 2

    def half_rows_of(owner):
        return pl.ds(pl.multiple_of(owner * shard + core * half_shard, half_shard), half_shard)

    source_rows = rows_of(core, half_shard)

    def gather_qkv(step):
        peer = (dp ^ (step + 1), me)
        remote(
            qkv_in.at[:, source_rows, :],
            land_qkv.at[:, half_rows_of(dp), :],
            gather_send.at[1],
            share_sem.at[0, step],
            peer,
        )

    def gather_out(step):
        peer = (dp ^ (step + 1), me)
        remote(
            out_in.at[source_rows, :],
            land_out.at[half_rows_of(dp), :],
            gather_send.at[2],
            share_sem.at[1, step],
            peer,
        )

    def hand_qkv(step):
        rows = half_rows_of(dp ^ (step + 1))
        part = land_qkv.at[:, rows, :]
        wait_bytes(part, share_sem.at[0, step])
        remote(part, part, share_send.at[0], gather_recv.at[1], partner)

    def hand_out(step):
        rows = half_rows_of(dp ^ (step + 1))
        part = land_out.at[rows, :]
        wait_bytes(part, share_sem.at[1, step])
        remote(part, part, share_send.at[1], gather_recv.at[2], partner)

    loop(n_dp - 1, gather_small)
    loop(n_dp - 1, gather_qkv)
    loop(n_dp - 1, gather_out)
    own_small = local_copy(small_own, small_land.at[dp], local_sem.at[0])

    def load_qkv(target, sem):
        local_copy(qkv_in, target.at[:, own_rows, :], sem)

        def one(step):
            rows = rows_of(dp ^ (step + 1), shard)
            local_copy(land_qkv.at[:, rows, :], target.at[:, rows, :], sem)

        loop(n_dp - 1, one)
        wait_bytes(target, sem)

    def load_out(target, sem):
        local_copy(out_in, target.at[own_rows, :], sem)

        def one(step):
            rows = rows_of(dp ^ (step + 1), shard)
            local_copy(land_out.at[rows, :], target.at[rows, :], sem)

        loop(n_dp - 1, one)
        wait_bytes(target, sem)

    half_ex, quarter_ex = n_ex // 2, n_ex // 4
    half_slots = half_ex * capacity
    side, quarter, rank = me // half_ex, me // quarter_ex, lax.rem(me, quarter_ex)
    first_ex = side * half_ex
    far_ex = (1 - side) * half_ex
    own_index = me - first_ex
    is_hub = (quarter == 1) | (quarter == 2)
    hub = (2 - side) * quarter_ex + rank
    hub_slot = lax.rem(quarter, 2)

    def served(slot):
        return far_ex + slot * quarter_ex + rank

    def block_of(area, index):
        return send.at[area, rows_of(index, capacity), :]

    def wait_blocks(sem, count):
        wait_bytes(send.at[0, pl.ds(0, count * capacity), :], sem)

    def land_block(kind, micro, index):
        return land.at[kind, micro, rows_of(index, capacity), :]

    def near_wait(sems, kind, micro):
        wait_blocks(sems.at[kind, micro], half_ex - 1)

    def far_wait(sems, kind, micro):
        @pl.when(is_hub)
        def _():
            wait_blocks(sems.at[kind, micro], half_ex - 2)

        @pl.when(jnp.logical_not(is_hub))
        def _():
            wait_blocks(sems.at[kind, micro], half_ex)

    def relay_wait(kind, micro):
        @pl.when(is_hub)
        def _():
            wait_blocks(far_send.at[kind, micro], 2 * (half_ex - 1))

    def pack(spot, spot_start, source, area, area_start):
        rows = pl.ds(spot_start, half_slots)
        send[area, pl.ds(area_start, half_slots), :] = dot(spot[rows, :], source[...]).astype(low)

    def spread(area, start, kind, micro, source, send_sem, recv_sem, own_sem):
        def one(step):
            peer = me ^ (step + 1)
            remote(
                block_of(area, start + peer - first_ex),
                land_block(kind, micro, source),
                send_sem,
                recv_sem,
                (dp, peer),
            )

        loop(half_ex - 1, one)
        local_copy(block_of(area, start + own_index), land_block(kind, micro, source), own_sem)

    def scatter_full(kind, micro, source):
        remote(
            source,
            hub_rows.at[kind, micro, hub_slot],
            full_send.at[kind, micro],
            full_recv.at[kind, micro, hub_slot],
            (dp, hub),
        )

    def scatter_near(kind, micro, source):
        area = MB + micro
        pack(place.at[micro], pl.multiple_of(first_ex * capacity, half_slots), source, area, 0)
        spread(
            area,
            0,
            kind,
            micro,
            me,
            ex_send.at[kind, micro],
            ex_recv.at[kind, micro],
            own_near.at[kind, micro],
        )

    def relay(kind, micro):
        @pl.when(is_hub)
        def _():
            if kind == KIND_ROW:
                wait_blocks(far_send.at[KIND_COT, micro], 2 * (half_ex - 1))
                wait_blocks(own_far.at[KIND_COT, micro], 2)

            def fetch(slot):
                wait_bytes(hub_rows.at[kind, micro, slot], full_recv.at[kind, micro, slot])
                local_copy(
                    hub_rows.at[kind, micro, slot],
                    hub_buf.at[slot, pl.ds(0, TOK_PAD), :],
                    hub_sem.at[slot],
                )

            def one(slot):
                rows = hub_buf.at[slot, pl.ds(0, TOK_PAD), :]
                wait_bytes(rows, hub_sem.at[slot])
                pack(
                    place_far.at[micro, slot],
                    0,
                    rows,
                    micro,
                    pl.multiple_of(slot * half_slots, half_slots),
                )
                spread(
                    micro,
                    slot * half_ex,
                    kind,
                    micro,
                    served(slot),
                    far_send.at[kind, micro],
                    far_recv.at[kind, micro],
                    own_far.at[kind, micro],
                )

            loop(2, fetch)
            loop(2, one)

    def gather(kind, micro, area):
        def to_hub(step):
            source = far_ex + step
            slot = lax.rem(source // quarter_ex, 2)
            target = hub_blocks.at[kind - KIND_BACK, micro, slot, rows_of(own_index, capacity), :]
            device = (1 + side) * quarter_ex + lax.rem(source, quarter_ex)

            @pl.when(device == me)
            def _():
                local_copy(block_of(area, source), target, own_hub.at[kind - KIND_BACK, micro, slot])

            @pl.when(device != me)
            def _():
                remote(
                    block_of(area, source),
                    target,
                    far_send.at[kind, micro],
                    hub_recv.at[kind - KIND_BACK, micro, slot],
                    (dp, device),
                )

        def to_near(step):
            peer = me ^ (step + 1)
            remote(
                block_of(area, peer),
                land_block(kind, micro, own_index),
                ex_send.at[kind, micro],
                ex_recv.at[kind, micro],
                (dp, peer),
            )

        loop(half_ex, to_hub)
        loop(half_ex - 1, to_near)
        local_copy(
            block_of(area, me), land_block(kind, micro, own_index), own_near.at[kind, micro]
        )

    def hub_sum(kind, micro):
        index = kind - KIND_BACK

        @pl.when(is_hub)
        def _():
            def fetch(slot):
                if kind == KIND_MADE:
                    wait_bytes(hub_sums.at[micro, slot], sum_send.at[0, micro, slot])
                wait_blocks(hub_recv.at[index, micro, slot], half_ex - 1)
                wait_blocks(own_hub.at[index, micro, slot], 1)
                local_copy(hub_blocks.at[index, micro, slot], hub_buf.at[slot], hub_sem.at[slot])

            def one(slot):
                wait_bytes(hub_buf.at[slot], hub_sem.at[slot])
                hub_sums[micro, slot] = dot(place_far[micro, slot], hub_buf[slot], TN).astype(low)
                remote(
                    hub_sums.at[micro, slot],
                    far_land.at[index, micro],
                    sum_send.at[index, micro, slot],
                    sum_recv.at[index, micro],
                    (dp, served(slot)),
                )

            loop(2, fetch)
            loop(2, one)

    def fetch_gathered(kind, micro, arrived, sem):
        near_wait(ex_recv, kind, micro)
        wait_blocks(own_near.at[kind, micro], 1)
        index = kind - KIND_BACK
        wait_bytes(far_land.at[index, micro], sum_recv.at[index, micro])
        near = arrived.at[pl.ds(0, half_slots), :]
        far = arrived.at[pl.ds(half_slots, TOK_PAD), :]
        local_copy(land.at[kind, micro, pl.ds(0, half_slots), :], near, sem)
        local_copy(far_land.at[index, micro], far, sem)
        wait_bytes(arrived.at[pl.ds(0, half_slots + TOK_PAD), :], sem)

    def gathered(micro, arrived, cols):
        spot = place.at[micro, pl.ds(pl.multiple_of(first_ex * capacity, half_slots), half_slots)]
        near = arrived[pl.ds(0, half_slots), cols]
        far = arrived[pl.ds(half_slots, TOK_PAD), cols]
        return dot(spot[...], near, TN) + far.astype(wide)

    def exchange_small(source, target, kind, micro):
        def one(step):
            peer = me ^ (step + 1)
            remote(
                source.at[micro, peer],
                target.at[micro, me],
                ex_send.at[kind, micro],
                ex_recv.at[kind, micro],
                (dp, peer),
            )

        loop(n_ex - 1, one)
        target[micro, me] = source[micro, me]

    def await_small(sems, ref, kind, micro):
        wait_bytes(ref.at[micro, pl.ds(0, n_ex - 1)], sems.at[kind, micro])

    def forward(wqkv, wout, tok, cot, raw, buffer, probs, qkv, first, mixed, resid, spill_sem):
        def spills(micro):
            tokens = rows_of(micro, TOK_PAD)
            pairs = [
                (probs.at[micro], spill_probs.at[micro]),
                (qkv.at[micro], spill_qkv.at[micro]),
                (first.at[tokens], spill_rows.at[0, tokens]),
                (mixed.at[tokens], spill_rows.at[1, tokens]),
                (resid.at[micro], spill_resid.at[micro]),
            ]
            return [
                pltpu.make_async_copy(source, target, spill_sem.at[micro, index])
                for index, (source, target) in enumerate(pairs)
            ]

        local_copy(cot_in, raw, local_sem.at[3]).wait()
        spread_rows(raw, buffer, cot)
        keep_cot = local_copy(cot, spill_cot, spill_sem.at[MB, 1])
        load = local_copy(tok_in, raw, local_sem.at[3])
        numbers = route_in[...].astype(wide)
        fill = jnp.full((2, SEQ_PAD - SEQ), -1.0, wide)
        for micro in range(MB):
            pieces = []
            for image in range(IMG_DEV):
                start = micro * TOK_MB + image * SEQ
                pieces += [numbers[:, start : start + SEQ], fill]
            route[micro] = jnp.concatenate(pieces, axis=1).astype(jnp.int32)

        remote(
            route, route_far.at[hub_slot], route_recv.at[2], route_recv.at[hub_slot], (dp, hub)
        )
        keep_cot.wait()

        def send_cot(micro):
            scatter_full(KIND_COT, micro, spill_cot.at[micro])
            scatter_near(KIND_COT, micro, cot.at[micro])

        def place_own(micro):
            place_tokens(
                route.at[micro], capacity, named.at[micro], place.at[micro], 0, n_ex
            )

        own_small.wait()
        loop(MB, place_own)
        send_cot(0)

        @pl.when(is_hub)
        def _():
            def one(index):
                micro, slot = index // 2, lax.rem(index, 2)
                place_tokens(
                    route_far.at[slot, micro],
                    capacity,
                    named_far,
                    place_far.at[micro, slot],
                    first_ex,
                    half_ex,
                )

            for slot in range(2):
                wait_bytes(route, route_recv.at[slot])
            loop(2 * MB, one)

        load.wait()
        spread_rows(raw, buffer, tok)
        tops[...] = jnp.full(tops.shape, -jnp.inf, wide)
        wait_bytes(small_land.at[pl.ds(0, n_dp - 1)], gather_recv.at[0])
        for owner in range(n_dp):
            small_t[:, owner * shard : (owner + 1) * shard] = small_land[owner, :, 0:shard]
        router_low[...] = small_t[pl.ds(0, n_ex), :].astype(low)
        gains[...] = small_t[pl.ds(n_ex, 8), :]
        keep_tok = local_copy(tok, spill_tok, spill_sem.at[MB, 0])
        loop(n_dp - 1, hand_qkv)
        wait_bytes(land_qkv.at[:, pl.ds(0, (D - shard) // 2), :], gather_recv.at[1])
        load_qkv(wqkv, local_sem.at[1])

        def out_arrives():
            loop(n_dp - 1, hand_out)

        def out_there():
            wait_bytes(land_out.at[pl.ds(0, (D - shard) // 2), :], gather_recv.at[2])
            load_out(wout, local_sem.at[1])

        def one(micro):
            attention_forward(
                tok.at[micro],
                gains,
                wqkv,
                wout,
                first.at[rows_of(micro, TOK_PAD)],
                qkv.at[micro],
                probs.at[micro],
                mixed.at[rows_of(micro, TOK_PAD)],
                resid.at[micro],
                second.at[rows_of(micro, TOK_PAD)],
                tops,
                lambda: pl.when(micro == 0)(out_arrives),
                lambda: pl.when(micro == 0)(out_there),
            )
            for copy in spills(micro):
                copy.start()
            rows = second.at[rows_of(micro, TOK_PAD)]
            gate_tokens(rows, router_low, named.at[micro], gate.at[micro])
            gate_slots(gate.at[micro], place.at[micro], capacity, gate_send.at[micro])
            exchange_small(gate_send, gate_land, KIND_GATE, micro)
            scatter_full(KIND_ROW, micro, rows)
            near_wait(ex_send, KIND_COT, micro)
            wait_blocks(own_near.at[KIND_COT, micro], 1)
            scatter_near(KIND_ROW, micro, rows)

            @pl.when(micro == 0)
            def _():
                send_cot(1)
                relay(KIND_COT, 0)


        loop(MB, one)

        def spread_top(step):
            peer = me ^ (step + 1)
            remote(tops, tops_land.at[me], red_send.at[0], red_recv.at[0], (dp, peer))

        loop(n_ex - 1, spread_top)
        tops_land[me] = tops[...]
        for micro in range(MB):
            for copy in spills(micro):
                copy.wait()
        keep_tok.wait()

    pl.run_scoped(
        forward,
        pltpu.VMEM((3, D, D), low),
        pltpu.VMEM((D, D), low),
        pltpu.VMEM((MB, TOK_PAD, D), low),
        pltpu.VMEM((MB, TOK_PAD, D), low),
        pltpu.VMEM((MB * TOK_MB, D), low),
        pltpu.VMEM((MB * TOK_MB + SEQ_PAD - SEQ + 1, D), wide),
        pltpu.VMEM((MB, IMG_DEV * HEADS, SEQ_PAD, SEQ_PAD), low),
        pltpu.VMEM((MB, 3, TOK_PAD, D), low),
        pltpu.VMEM((MB * TOK_PAD, D), low),
        pltpu.VMEM((MB * TOK_PAD, D), low),
        pltpu.VMEM((MB, TOK_PAD, D), wide),
        pltpu.SemaphoreType.DMA((MB + 1, 5)),
    )

    def experts(w_in, w_out, rows_in, cot, grad_rows, rows_t, grad_t, hidden, grad_pre, made, sems):
        eye = lax.broadcasted_iota(jnp.int32, (capacity, capacity), 0) == lax.broadcasted_iota(
            jnp.int32, (capacity, capacity), 1
        )

        def gate_column(micro, source):
            row = gate_land[micro, source, 0:1, 0:capacity]
            return jnp.sum(jnp.where(eye, row, 0.0), axis=1, keepdims=True)

        loads = [
            local_copy(expert_in, w_in, local_sem.at[4]),
            local_copy(expert_out, w_out, local_sem.at[5]),
        ]
        relay(KIND_ROW, 0)
        for copy in loads:
            copy.wait()

        def one(micro):
            pl.when(micro > 0)(lambda: relay(KIND_ROW, micro))
            near_wait(ex_recv, KIND_COT, micro)
            far_wait(far_recv, KIND_COT, micro)
            await_small(ex_recv, gate_land, KIND_GATE, micro)
            near_wait(ex_recv, KIND_ROW, micro)
            far_wait(far_recv, KIND_ROW, micro)
            wait_blocks(own_near.at[KIND_ROW, micro], 1)

            @pl.when(is_hub)
            def _():
                wait_blocks(own_far.at[KIND_ROW, micro], 2)

            load_rows = local_copy(land.at[KIND_ROW, micro], rows_in, sems.at[0])
            load_cot = local_copy(land.at[KIND_COT, micro], cot, sems.at[1])
            load_rows.wait()
            load_cot.wait()

            def scale(source):
                rows = rows_of(source, capacity)
                wide_cot = cot[rows, :].astype(wide)
                grad_rows[rows, :] = (wide_cot * gate_column(micro, source)).astype(low)

            loop(n_ex, scale)

            def turn(index):
                rows = rows_of(index, 128)
                cols = pl.ds(pl.multiple_of(micro * slots + index * 128, 128), 128)
                rows_t[:, cols] = rows_in[rows, :].T
                grad_t[:, cols] = grad_rows[rows, :].T

            loop(slots // 128, turn)

            @pl.when(micro > 0)
            def _():
                pltpu.make_async_copy(hidden, spill_hidden, sems.at[2]).wait()
                pltpu.make_async_copy(grad_pre, spill_grad, sems.at[3]).wait()

            def through(index):
                cols = rows_of(index // (slots // BLOCK_ROWS), BLOCK_FF)
                rows = rows_of(index % (slots // BLOCK_ROWS), BLOCK_ROWS)
                value, slope = gelu_both(dot(rows_in[rows, :], w_in[:, cols]))
                hidden[rows, cols] = value.astype(low)
                grad_hidden = dot(grad_rows[rows, :], w_out[cols, :], NT)
                grad_pre[rows, cols] = (grad_hidden * slope).astype(low)

            loop((FF // BLOCK_FF) * (slots // BLOCK_ROWS), through, 2)

            @pl.when(micro < MB - 1)
            def _():
                local_copy(hidden, spill_hidden, sems.at[2])
                local_copy(grad_pre, spill_grad, sems.at[3])

            relay_wait(KIND_ROW, micro)

            def back(index):
                rows = rows_of(index, BLOCK_ROWS)
                send[micro, rows, :] = dot(grad_pre[rows, :], w_in[...], NT).astype(low)

            loop(slots // BLOCK_ROWS, back)
            gather(KIND_BACK, micro, micro)
            near_wait(ex_send, KIND_ROW, micro)

            def forth(index):
                rows = rows_of(index, MADE_ROWS)
                made[...] = dot(hidden[rows, :], w_out[...])
                count = MADE_ROWS // capacity

                def finish(part):
                    source = index * count + part
                    own = rows_of(source, capacity)
                    values = made[rows_of(part, capacity), :]
                    column = jnp.sum(values * cot[own, :].astype(wide), axis=1, keepdims=True)
                    slope_send[micro, source, 0:1, 0:capacity] = jnp.sum(
                        jnp.where(eye, column, 0.0), axis=0, keepdims=True
                    )
                    send[MB + micro, own, :] = (values * gate_column(micro, source)).astype(low)

                loop(count, finish)

            loop(slots // MADE_ROWS, forth)
            exchange_small(slope_send, slope_land, KIND_SLOPE, micro)
            pl.when(micro == 0)(lambda: relay(KIND_COT, 1))

        loop(MB, one)

        def send_made(micro):
            gather(KIND_MADE, micro, MB + micro)

        hub_sum(KIND_BACK, 0)
        loop(MB, send_made)

        wait_bytes(tops_land.at[pl.ds(0, n_ex - 1)], red_recv.at[0])
        wait_bytes(tops_land.at[pl.ds(0, n_ex - 1)], red_send.at[0])
        tops[...] = jnp.max(tops_land[...], axis=0)

    def expert_phase(
        w_in, w_out, rows_in, cot, grad_rows, rows_t, grad_t, hidden, grad_pre, made, sems
    ):
        experts(w_in, w_out, rows_in, cot, grad_rows, rows_t, grad_t, hidden, grad_pre, made, sems)
        weight_grads(rows_t, grad_t, hidden, grad_pre)
        hub_sum(KIND_BACK, 1)

    def weight_grads(rows_t, grad_t, hidden, grad_pre):
        blocks = FF // GRAD_FF
        half = pl.ds(0, slots)
        other = pl.ds(slots, slots)

        def scoped(kept_hidden, kept_grad, out_in, out_out, load_sems, store_sems):
            def fetch(block, slot):
                cols = rows_of(block, GRAD_FF)
                local_copy(spill_hidden.at[:, cols], kept_hidden.at[slot], load_sems.at[0, slot])
                local_copy(spill_grad.at[:, cols], kept_grad.at[slot], load_sems.at[1, slot])

            def stored(block, slot):
                cols = rows_of(block, GRAD_FF)
                return (
                    pltpu.make_async_copy(
                        out_in.at[slot], stage_in.at[:, cols], store_sems.at[0, slot]
                    ),
                    pltpu.make_async_copy(
                        out_out.at[slot], stage_out.at[:, cols], store_sems.at[1, slot]
                    ),
                    pltpu.make_async_copy(
                        out_in.at[slot, own_rows, :],
                        share_in.at[dp, :, cols],
                        store_sems.at[2, slot],
                    ),
                )

            def ship(block, slot):
                for copy in stored(block, slot):
                    copy.wait()
                cols = rows_of(block, GRAD_FF)

                def one(step):
                    peer = dp ^ (step + 1)
                    remote(
                        stage_in.at[rows_of(peer, shard), cols],
                        share_in.at[dp, :, cols],
                        rs_send.at[0],
                        rs_recv.at[0],
                        (peer, me),
                    )

                loop(n_dp - 1, one)

            fetch(0, 0)

            def one(block):
                slot = lax.rem(block, 2)

                @pl.when(block + 1 < blocks)
                def _():
                    fetch(block + 1, 1 - slot)

                wait_bytes(kept_hidden.at[slot], load_sems.at[0, slot])
                wait_bytes(kept_grad.at[slot], load_sems.at[1, slot])
                cols = rows_of(block, GRAD_FF)
                out_in[slot] = (
                    dot(rows_t[:, half], kept_grad[slot]) + dot(rows_t[:, other], grad_pre[:, cols])
                ).astype(low)
                out_out[slot] = (
                    dot(grad_t[:, half], kept_hidden[slot]) + dot(grad_t[:, other], hidden[:, cols])
                ).astype(low)
                for copy in stored(block, slot):
                    copy.start()

                @pl.when(block > 0)
                def _():
                    ship(block - 1, 1 - slot)

            loop(blocks, one)
            ship(blocks - 1, (blocks - 1) % 2)

        pl.run_scoped(
            scoped,
            pltpu.VMEM((2, slots, GRAD_FF), low),
            pltpu.VMEM((2, slots, GRAD_FF), low),
            pltpu.VMEM((2, D, GRAD_FF), low),
            pltpu.VMEM((2, D, GRAD_FF), low),
            pltpu.SemaphoreType.DMA((2, 2)),
            pltpu.SemaphoreType.DMA((3, 2)),
        )

    pl.run_scoped(
        expert_phase,
        pltpu.VMEM((D, FF), low),
        pltpu.VMEM((FF, D), low),
        pltpu.VMEM((slots, D), low),
        pltpu.VMEM((slots, D), low),
        pltpu.VMEM((slots, D), low),
        pltpu.VMEM((D, MB * slots), low),
        pltpu.VMEM((D, MB * slots), low),
        pltpu.VMEM((slots, FF), low),
        pltpu.VMEM((slots, FF), low),
        pltpu.VMEM((MADE_ROWS, D), wide),
        pltpu.SemaphoreType.DMA((4,)),
    )

    width = FF // n_dp

    def ship_out(step):
        peer = dp ^ (step + 1)
        remote(
            stage_out.at[:, rows_of(peer, width)],
            share_out.at[dp],
            rs_send.at[1],
            rs_recv.at[1],
            (peer, me),
        )

    def spread_tops(step):
        peer = dp ^ (step + 1)
        remote(tops, tops_dp.at[dp], red_send.at[1], red_recv.at[1], (peer, me))

    loop(n_dp - 1, spread_tops)
    tops_dp[dp] = tops[...]

    chips = parts = n_ex // 2
    part_rows = part_size(n_dp, n_ex)
    z = me // 2

    def backward(
        wqkv,
        wout,
        resid,
        cot,
        probs,
        qkv,
        first,
        mixed,
        arrived,
        grad,
        attended,
        proj,
        result,
        out,
        grads,
        pairs,
        part_own,
        buffer,
        compact,
        sems,
    ):
        first_loads = [
            local_copy(source, target, sems.at[index])
            for index, (source, target) in enumerate(
                [
                    (spill_rows.at[0], first),
                    (spill_rows.at[1], mixed),
                    (spill_resid, resid),
                ]
            )
        ]
        kept_out = arrived.at[pl.ds(0, D), pl.ds(0, width)]
        local_copy(stage_out.at[:, rows_of(dp, width)], kept_out, sems.at[5]).wait()
        local_copy(kept_out, share_out.at[dp], sems.at[5]).wait()
        gain_sums[...] = jnp.zeros(gain_sums.shape, wide)
        small_sum[...] = jnp.zeros(small_sum.shape, wide)
        for copy in first_loads:
            copy.wait()
        load_qkv(wqkv, sems.at[4])
        load_out(wout, sems.at[4])

        def own_half(which):
            return pl.ds(pl.multiple_of(which * half_shard, half_shard), half_shard)

        def to_partner(part):
            remote(
                grads.at[part, :, own_half(1 - core), :],
                pair_land.at[part],
                pair_send.at[part],
                pair_recv.at[part],
                partner,
            )

        def to_owners(part):
            wait_bytes(pair_land.at[part], pair_recv.at[part])
            local_copy(pair_land.at[part], pairs.at[part], sems.at[5]).wait()

            def add_pair(owner):
                mine = grads[part, owner, own_half(core), :].astype(wide)
                pairs[part, owner] = (mine + pairs[part, owner].astype(wide)).astype(low)

            loop(n_dp, add_pair)

            def one(step):
                peer = dp ^ (step + 1)
                remote(
                    pairs.at[part, peer],
                    dp_land.at[dp, own_half(part), :],
                    own_send.at[part],
                    own_recv.at[part],
                    (peer, me),
                )

            loop(n_dp - 1, one)

        def grad_block(part, left, right):
            def one(block):
                cols = rows_of(block, COLS)
                value = dot(left[...], right[:, cols], TN).astype(low)
                for owner in range(n_dp):
                    grads[part, owner, :, cols] = value[owner * shard : (owner + 1) * shard, :]

            loop(D // COLS, one)
            to_partner(part)

        def one(micro):
            tokens = rows_of(micro, TOK_PAD)
            loads = [
                local_copy(spill_probs.at[micro], probs, sems.at[0]),
                local_copy(spill_qkv.at[micro], qkv, sems.at[1]),
                local_copy(spill_cot.at[micro], cot, sems.at[2]),
            ]
            await_small(ex_recv, slope_land, KIND_SLOPE, micro)
            fetch_gathered(KIND_BACK, micro, arrived, sems.at[3])
            row = jnp.concatenate(
                [slope_land[micro, expert, 0:1, 0:capacity] for expert in range(n_ex)], axis=1
            )
            blocks = jnp.where(own_columns(n_ex, capacity), row, 0.0)
            slope = exact_dot(blocks, place[micro], NN)
            gates = gate[micro]
            grad_logits = gates * (slope - jnp.sum(gates * slope, axis=0, keepdims=True))
            grad_logits = grad_logits.astype(low)
            small_sum[pl.ds(0, n_ex), :] += dot(grad_logits, second[tokens, :])
            for block in range(D // COLS):
                cols = pl.ds(block * COLS, COLS)
                grad[micro, :, cols] = gathered(micro, arrived, cols) + dot(
                    grad_logits, router_low[:, cols], TN
                )
            for load in loads:
                load.wait()
            backward_scores(
                gains,
                wout,
                qkv,
                probs,
                resid.at[micro],
                grad.at[micro],
                attended.at[tokens],
                proj.at[:, tokens, :],
                out,
                gain_sums,
                cot,
                lambda: pl.when(micro == MB - 1)(lambda: grad_block(3, mixed, attended)),
            )
            pl.when(micro == 0)(lambda: loop(2, ship_out))

        loop(MB, one)
        to_owners(3)
        hub_sum(KIND_MADE, 0)
        for part in range(3):
            grad_block(part, first, proj.at[part])
        for part in range(3):
            to_owners(part)
        loop(n_dp - 3, lambda step: ship_out(step + 2))
        hub_sum(KIND_MADE, 1)

        def finish(micro):
            local_copy(spill_tok.at[micro], cot, sems.at[2]).wait()
            backward_input(
                cot,
                gains,
                wqkv,
                grad.at[micro],
                proj.at[:, rows_of(micro, TOK_PAD), :],
                gain_sums,
                result,
            )

        loop(MB, finish)
        small_sum[n_ex : n_ex + 1, :] = jnp.sum(gain_sums[0], axis=0, keepdims=True)
        small_sum[n_ex + 1 : n_ex + 2, :] = jnp.sum(gain_sums[1], axis=0, keepdims=True)
        remote(small_sum, small_pair, red_send.at[3], red_recv.at[3], partner)
        compact_rows(grad, buffer, compact)
        store = local_copy(compact, grad_input, sems.at[4])
        wait_bytes(small_pair, red_recv.at[3])
        both = small_sum[...] + small_pair[...]
        small_cut[...] = jnp.zeros(small_cut.shape, wide)
        for owner in range(n_dp):
            small_cut[owner, :, 0:shard] = both[:, owner * shard : (owner + 1) * shard]

        def small_to_owner(step):
            peer = dp ^ (step + 1)
            remote(
                small_cut.at[peer], small_dp.at[dp], red_send.at[5], red_recv.at[5], (peer, me)
            )

        loop(n_dp - 1, small_to_owner)
        small_dp[dp] = small_cut[dp]
        for part in range(4):
            wait_bytes(dp_land.at[pl.ds(0, n_dp - 1), own_half(part), :], own_recv.at[part])
            result[pl.ds(part * half_shard, half_shard), :] = pairs[part, dp].astype(wide)

        def load_dp(step):
            peer = dp ^ (step + 1)
            local_copy(dp_land.at[peer], proj_rows(step), sems.at[0])

        def proj_rows(step):
            return proj.at[lax.rem(step, 3), rows_of(step // 3, 2 * shard), :]

        loop(n_dp - 1, load_dp)
        wait_bytes(dp_land.at[pl.ds(0, n_dp - 1)], sems.at[0])

        def add_dp(step):
            result[pl.ds(0, 2 * shard), :] += proj_rows(step)[...].astype(wide)

        loop(n_dp - 1, add_dp)
        total = parts * part_rows
        if total > 2 * shard:
            result[pl.ds(2 * shard, total - 2 * shard), :] = jnp.zeros(
                (total - 2 * shard, D), wide
            )
        grad_low = arrived
        grad_low[pl.ds(0, total), :] = result[pl.ds(0, total), :].astype(low)

        def chip(index):
            return (dp, 2 * index + core)

        def to_part(step):
            peer = z ^ (step + 1)
            remote(
                grad_low.at[rows_of(peer, part_rows), :],
                part_land.at[z],
                red_send.at[6],
                red_recv.at[6],
                chip(peer),
            )

        loop(parts - 1, to_part)
        wait_bytes(small_dp.at[pl.ds(0, n_dp - 1)], red_recv.at[5])
        small_part[me] = jnp.sum(small_dp[...], axis=0)

        def to_chip(step):
            remote(
                small_part.at[me],
                small_part.at[me],
                red_send.at[7],
                red_recv.at[7],
                chip(z ^ (step + 1)),
            )

        loop(parts - 1, to_chip)
        mine = rows_of(z, part_rows)
        result[pl.ds(0, part_rows), :] = grad_low[mine, :].astype(wide)
        wait_bytes(part_land.at[pl.ds(0, parts - 1)], red_recv.at[6])

        def load_part(step):
            peer = z ^ (step + 1)
            local_copy(part_land.at[peer], part_own.at[step], sems.at[0])

        loop(parts - 1, load_part)
        wait_bytes(part_own, sems.at[0])

        def add_part(step):
            result[pl.ds(0, part_rows), :] += part_own[step].astype(wide)

        loop(parts - 1, add_part)

        summed = out.at[pl.ds(0, part_rows), :]
        summed[...] = result[pl.ds(0, part_rows), :].astype(low)

        def to_all(step):
            remote(
                summed,
                share.at[core, mine, :],
                red_send.at[8],
                red_recv.at[8],
                chip(z ^ (step + 1)),
            )

        loop(parts - 1, to_all)
        local_copy(summed, share.at[core, mine, :], sems.at[0]).wait()
        wait_bytes(grad_low.at[pl.ds(0, (parts - 1) * part_rows), :], red_send.at[6])

        def combine(micro):
            fetch_gathered(KIND_MADE, micro, arrived, sems.at[3])
            for block in range(D // COLS):
                cols = pl.ds(block * COLS, COLS)
                grad[micro, :, cols] = resid[micro, :, cols] + gathered(micro, arrived, cols)

        loop(MB, combine)
        store.wait()
        compact_rows(grad, buffer, compact)
        store = local_copy(compact, layer_out, sems.at[4])
        wait_bytes(share.at[0, pl.ds(0, (parts - 1) * part_rows), :], red_recv.at[8])
        half_rows = pl.ds(0, 2 * shard)
        remote(
            share.at[core, half_rows, :],
            share.at[core, half_rows, :],
            red_send.at[9],
            red_recv.at[9],
            partner,
        )
        wait_bytes(small_part.at[pl.ds(0, parts - 1)], red_recv.at[7])
        chosen = small_part[core]
        for index in range(1, chips):
            chosen += small_part[2 * index + core]
        share_small[...] = chosen
        wait_bytes(tops_dp.at[pl.ds(0, n_dp - 1)], red_recv.at[1])
        tops_out[...] = jnp.max(tops_dp[...], axis=0)
        wait_bytes(share.at[0, half_rows, :], red_recv.at[9])
        store.wait()

        for part in range(4):
            wait_bytes(pair_land.at[part], pair_send.at[part])
            wait_bytes(dp_land.at[pl.ds(0, n_dp - 1), own_half(part), :], own_send.at[part])
        wait_bytes(grad_low.at[pl.ds(0, (parts - 1) * part_rows), :], red_send.at[8])

    pl.run_scoped(
        backward,
        pltpu.VMEM((3, D, D), low),
        pltpu.VMEM((D, D), low),
        pltpu.VMEM((MB, TOK_PAD, D), wide),
        pltpu.VMEM((TOK_PAD, D), low),
        pltpu.VMEM((IMG_DEV * HEADS, SEQ_PAD, SEQ_PAD), low),
        pltpu.VMEM((3, TOK_PAD, D), low),
        pltpu.VMEM((MB * TOK_PAD, D), low),
        pltpu.VMEM((MB * TOK_PAD, D), low),
        pltpu.VMEM((slots, D), low),
        pltpu.VMEM((MB, TOK_PAD, D), wide),
        pltpu.VMEM((MB * TOK_PAD, D), low),
        pltpu.VMEM((3, MB * TOK_PAD, D), low),
        pltpu.VMEM((TOK_PAD, D), wide),
        pltpu.VMEM((TOK_PAD, D), low),
        pltpu.VMEM((4, n_dp, shard, D), low),
        pltpu.VMEM((4, n_dp, half_shard, D), low),
        pltpu.VMEM((parts - 1, part_rows, D), low),
        pltpu.VMEM((MB * TOK_MB + SEQ_PAD - SEQ + 1, D), wide),
        pltpu.VMEM((MB * TOK_MB, D), low),
        pltpu.SemaphoreType.DMA((6,)),
    )

    wait_bytes(share_in.at[pl.ds(0, n_dp - 1)], rs_recv.at[0])
    wait_bytes(share_out.at[pl.ds(0, n_dp - 1)], rs_recv.at[1])
    wait_bytes(share_in.at[pl.ds(0, n_dp - 1)], rs_send.at[0])
    wait_bytes(share_out.at[pl.ds(0, n_dp - 1)], rs_send.at[1])
    wait_bytes(small_land.at[pl.ds(0, n_dp - 1)], gather_send.at[0])
    wait_bytes(small_pair, red_send.at[3])
    others_half = pl.ds(0, (D - shard) // 2)
    for sems in (gather_send.at[1], share_send.at[0]):
        wait_bytes(land_qkv.at[:, others_half, :], sems)
    for sems in (gather_send.at[2], share_send.at[1]):
        wait_bytes(land_out.at[others_half, :], sems)
    wait_bytes(route, route_recv.at[2])
    for micro in range(MB):
        for kind in (KIND_COT, KIND_ROW):
            wait_bytes(spill_cot.at[micro], full_send.at[kind, micro])
        for kind in (KIND_BACK, KIND_MADE):
            near_wait(ex_send, kind, micro)
            far_wait(far_send, kind, micro)
        await_small(ex_send, gate_land, KIND_GATE, micro)
        await_small(ex_send, slope_land, KIND_SLOPE, micro)
    wait_bytes(tops_dp.at[pl.ds(0, n_dp - 1)], red_send.at[1])

    @pl.when(is_hub)
    def _():
        for micro in range(MB):
            for slot in range(2):
                wait_bytes(hub_sums.at[micro, slot], sum_send.at[1, micro, slot])

    wait_bytes(small_dp.at[pl.ds(0, n_dp - 1)], red_send.at[5])
    wait_bytes(small_part.at[pl.ds(0, parts - 1)], red_send.at[7])
    wait_bytes(share.at[0, pl.ds(0, 2 * shard), :], red_send.at[9])


def part_size(n_dp, n_ex):
    shard, parts = D // n_dp, n_ex // 2
    return -(-2 * shard // (parts * 16)) * 16


def run_block(n_dp, n_ex, capacity, operands):
    shard, slots = D // n_dp, n_ex * capacity
    parts, part_rows = n_ex // 2, part_size(n_dp, n_ex)
    total = parts * part_rows
    lanes = -(-shard // 128) * 128
    outs = [
        ((MB * TOK_MB, D), low),
        ((MB * TOK_MB, D), low),
        ((2, total, D), low),
        ((n_ex + 8, lanes), wide),
        ((n_dp, shard, FF), low),
        ((n_dp, D, FF // n_dp), low),
        ((16, 128), wide),
        ((4, MB, slots, D), low),
        ((slots, FF), low),
        ((slots, FF), low),
        ((MB, IMG_DEV * HEADS, SEQ_PAD, SEQ_PAD), low),
        ((MB, 3, TOK_PAD, D), low),
        ((2, MB * TOK_PAD, D), low),
        ((MB, TOK_PAD, D), low),
        ((MB, TOK_PAD, D), low),
        ((MB, TOK_PAD, D), wide),
        ((3, D, D), low),
        ((D, D), low),
        ((2, MB, 2, TOK_PAD, D), low),
        ((2, MB, 2, slots // 2, D), low),
        ((2, MB, TOK_PAD, D), low),
        ((D, FF), low),
        ((D, FF), low),
        ((4, n_dp, shard // 2, D), low),
        ((n_dp, 2 * shard, D), low),
        ((parts, part_rows, D), low),
    ]
    in_vmem = (3, 6)
    return pl.pallas_call(
        functools.partial(block_kernel, n_dp, n_ex, capacity),
        out_shape=[jax.ShapeDtypeStruct(*one) for one in outs],
        in_specs=[ANY, ANY, VMEM, ANY, ANY, VMEM, VMEM, ANY, ANY],
        out_specs=[VMEM if index in in_vmem else ANY for index in range(len(outs))],
        scratch_shapes=[
            pltpu.VMEM((MB, 2, TOK_PAD), jnp.int32),
            pltpu.VMEM((2, MB, 2, TOK_PAD), jnp.int32),
            pltpu.VMEM((n_ex + 8, lanes), wide),
            pltpu.VMEM((n_dp, n_ex + 8, lanes), wide),
            pltpu.VMEM((n_ex + 8, D), wide),
            pltpu.VMEM((n_ex, D), low),
            pltpu.VMEM((8, D), wide),
            pltpu.VMEM((MB * TOK_PAD, D), low),
            pltpu.VMEM((MB, slots, TOK_PAD), low),
            pltpu.VMEM((MB, 2, slots // 2, TOK_PAD), low),
            pltpu.VMEM((MB, n_ex, TOK_PAD), wide),
            pltpu.VMEM((n_ex, TOK_PAD), wide),
            pltpu.VMEM((MB, n_ex, TOK_PAD), wide),
            pltpu.VMEM((2 * MB, slots, D), low),
            pltpu.VMEM((2, slots // 2, D), low),
            pltpu.VMEM((MB, 2, TOK_PAD, D), low),
            pltpu.VMEM((MB, n_ex, 8, 128), wide),
            pltpu.VMEM((MB, n_ex, 8, 128), wide),
            pltpu.VMEM((MB, n_ex, 8, 128), wide),
            pltpu.VMEM((MB, n_ex, 8, 128), wide),
            pltpu.VMEM((16, 128), wide),
            pltpu.VMEM((n_ex, 16, 128), wide),
            pltpu.VMEM((n_dp, 16, 128), wide),
            pltpu.VMEM((n_ex + 8, D), wide),
            pltpu.VMEM((n_ex + 8, D), wide),
            pltpu.VMEM((n_dp, n_ex + 8, lanes), wide),
            pltpu.VMEM((n_dp, n_ex + 8, lanes), wide),
            pltpu.VMEM((n_ex, n_ex + 8, lanes), wide),
            pltpu.VMEM((2, 8, D), wide),
            pltpu.SemaphoreType.DMA((3,)),
            pltpu.SemaphoreType.DMA((3,)),
            pltpu.SemaphoreType.DMA((2,)),
            pltpu.SemaphoreType.DMA((2, n_dp - 1)),
            pltpu.SemaphoreType.DMA((6, MB)),
            pltpu.SemaphoreType.DMA((6, MB)),
            pltpu.SemaphoreType.DMA((4, MB)),
            pltpu.SemaphoreType.DMA((4, MB)),
            pltpu.SemaphoreType.DMA((2, MB)),
            pltpu.SemaphoreType.DMA((2, MB, 2)),
            pltpu.SemaphoreType.DMA((2, MB, 2)),
            pltpu.SemaphoreType.DMA((2, MB, 2)),
            pltpu.SemaphoreType.DMA((2, MB)),
            pltpu.SemaphoreType.DMA((3,)),
            pltpu.SemaphoreType.DMA((4, MB)),
            pltpu.SemaphoreType.DMA((2, MB)),
            pltpu.SemaphoreType.DMA((2, MB, 2)),
            pltpu.SemaphoreType.DMA((2,)),
            pltpu.SemaphoreType.DMA((2,)),
            pltpu.SemaphoreType.DMA((2,)),
            pltpu.SemaphoreType.DMA((10,)),
            pltpu.SemaphoreType.DMA((10,)),
            pltpu.SemaphoreType.DMA((4,)),
            pltpu.SemaphoreType.DMA((4,)),
            pltpu.SemaphoreType.DMA((4,)),
            pltpu.SemaphoreType.DMA((4,)),
            pltpu.SemaphoreType.DMA((6,)),
        ],
        compiler_params=pltpu.CompilerParams(
            collective_id=0, has_side_effects=True, vmem_limit_bytes=60 * 2**20
        ),
        name="encoder_block",
    )(*operands)


def per_device(
    tokens,
    attn_qkv,
    attn_out,
    router,
    norm_gains,
    expert_in,
    expert_out,
    routes,
    clip_limit,
    cotangent,
):
    n_dp, n_ex = lax.axis_size("dp"), lax.axis_size("expert")
    capacity = max(8, (TOK_MB * 10 // (4 * n_ex) + 7) // 8 * 8)
    shard = D // n_dp
    results = run_block(
        n_dp,
        n_ex,
        capacity,
        (
            tokens,
            cotangent,
            routes.T,
            attn_qkv,
            attn_out,
            router.T,
            norm_gains,
            expert_in[0],
            expert_out[0],
        ),
    )
    layer_out, grad_input, share, share_small, share_in, share_out, tops = results[:7]
    share = share[:, : 2 * shard].reshape(2, 4, shard // 2, D).astype(wide)
    share = jnp.swapaxes(share, 0, 1).reshape(4, shard, D)
    head_max = tops[:HEADS, 0]
    factor = clip_limit / jnp.maximum(head_max, clip_limit)
    root_scale = jnp.repeat(jnp.sqrt(factor), HEAD_DIM)
    clipped_qk = attn_qkv[:2].astype(wide) * root_scale[None, None, :]
    return (
        layer_out,
        grad_input,
        share[:3],
        share[3],
        share_small[:n_ex, :shard].T,
        share_small[n_ex : n_ex + 2, :shard],
        jnp.sum(share_in.astype(wide), axis=0)[None],
        jnp.sum(share_out.astype(wide), axis=0).T[None],
        head_max,
        clipped_qk,
    )


def solution(mesh):
    placed = (
        P(("dp", "expert"), None),
        P(None, "dp", None),
        P("dp", None),
        P("dp", None),
        P(None, "dp"),
        P("expert", None, None),
        P("expert", None, None),
        P(("dp", "expert"), None),
        P(),
        P(("dp", "expert"), None),
    )
    return jax.shard_map(
        per_device,
        mesh=mesh,
        in_specs=placed,
        out_specs=(
            P(("dp", "expert"), None),
            P(("dp", "expert"), None),
            P(None, "dp", None),
            P("dp", None),
            P("dp", None),
            P(None, "dp"),
            P("expert", "dp", None),
            P("expert", "dp", None),
            P(),
            P(None, "dp", None),
        ),
        check_vma=False,
    )
```

```python
import functools
import jax
import jax.numpy as jnp
from jax import lax
from jax.experimental import pallas as pl
from jax.experimental.pallas import tpu as pltpu
from jax.sharding import PartitionSpec as P

D = 768
HEADS = 12
HEAD_DIM = 64
FF = 3072
SEQ = 197
IMG_DEV = 2
MB = 2
TOK_MB = 394
SEQ_PAD = 208
TOK_PAD = IMG_DEV * SEQ_PAD
PAIRS = HEADS // 2
UNROLL = 6
COLS = 256

epsilon = 1e-06
qk_scale = 0.125
gelu_coeff = 0.7978845608028654
low = jnp.bfloat16
wide = jnp.float32

NN = (((1,), (0,)), ((), ()))
NT = (((1,), (1,)), ((), ()))
TN = (((0,), (0,)), ((), ()))


def dot(left, right, dims=NN):
    return lax.dot_general(left, right, dims, preferred_element_type=wide)


def rows_of(index, size):
    return pl.ds(pl.multiple_of(index * size, size), size)


def loop(count, body, unroll=1):
    def step(index, carry):
        body(index)
        return carry

    lax.fori_loop(0, count, step, 0, unroll=unroll)


def norm_parts(values_in):
    row_mean = jnp.sum(values_in, axis=-1, keepdims=True) * (1.0 / D)
    centred = values_in - row_mean
    row_var = jnp.sum(centred * centred, axis=-1, keepdims=True) * (1.0 / D)
    inverse = lax.rsqrt(row_var + epsilon)
    return centred * inverse, inverse


def norm_back(unit, inverse, gain_row, incoming):
    scaled = incoming * gain_row
    mean_one = jnp.sum(scaled, axis=-1, keepdims=True) * (1.0 / D)
    mean_two = jnp.sum(scaled * unit, axis=-1, keepdims=True) * (1.0 / D)
    return (scaled - mean_one - unit * mean_two) * inverse


def fold_rows(values_in):
    return jnp.sum(values_in.reshape(-1, 8, values_in.shape[-1]), axis=0)


def gelu_both(values_in):
    squared = values_in * values_in
    bent = jnp.tanh(values_in * (gelu_coeff + (gelu_coeff * 0.044715) * squared))
    half = 0.5 + 0.5 * bent
    slope = half + half * (1.0 - bent) * values_in * (
        gelu_coeff + (3.0 * 0.044715 * gelu_coeff) * squared
    )
    return values_in * half, slope


def head_mask(half):
    lane = lax.broadcasted_iota(jnp.int32, (1, 2 * HEAD_DIM), 1)
    return (lane // HEAD_DIM) == half


def attention_forward(
    tok, gains, wqkv, wout, first, qkv, probs, mixed, resid, second, tops, after_qkv, before_out
):
    def norm_one(index):
        rows = rows_of(index, TOK_PAD)
        unit, _ = norm_parts(tok[rows, :].astype(wide))
        first[rows, :] = (unit * gains[0:1, :]).astype(low)

    loop(1, norm_one)

    def project(index):
        part, cols = index // (D // COLS), rows_of(index % (D // COLS), COLS)
        qkv[part, :, cols] = dot(first[...], wqkv[part, :, cols]).astype(low)

    loop(3 * (D // COLS), project)
    after_qkv()

    def attend(index):
        image, pair = index // PAIRS, index % PAIRS
        rows, cols = rows_of(image, SEQ_PAD), rows_of(pair, 2 * HEAD_DIM)
        query, key, value = qkv[0, rows, cols], qkv[1, rows, cols], qkv[2, rows, cols]
        key_id = lax.broadcasted_iota(jnp.int32, (SEQ_PAD, SEQ_PAD), 1)
        row_id = lax.broadcasted_iota(jnp.int32, (SEQ_PAD, 1), 0)
        total = jnp.zeros((SEQ_PAD, 2 * HEAD_DIM), wide)
        for half in range(2):
            mask = head_mask(half)
            scores = dot(jnp.where(mask, query * qk_scale, 0.0).astype(low), key, NT)
            scores = jnp.where(key_id < SEQ, scores, -jnp.inf)
            row_top = jnp.max(scores, axis=-1, keepdims=True)
            exp_scores = jnp.exp(scores - row_top)
            attn = exp_scores * (1.0 / jnp.sum(exp_scores, axis=-1, keepdims=True))
            attn = attn.astype(low)
            probs[2 * index + half] = attn
            total += dot(attn, jnp.where(mask, value, 0.0).astype(low))
            top = jnp.max(jnp.where(row_id < SEQ, row_top, -jnp.inf), axis=0, keepdims=True)
            slot = pl.ds(2 * pair + half, 1)
            tops[slot, :] = jnp.maximum(tops[slot, :], jnp.broadcast_to(top, (1, 128)))
        mixed[rows, cols] = total.astype(low)

    loop(IMG_DEV * PAIRS, attend, UNROLL)
    before_out()

    def add_out(index):
        cols = rows_of(index, COLS)
        resid[:, cols] = tok[:, cols].astype(wide) + dot(mixed[...], wout[:, cols])

    loop(D // COLS, add_out)

    def norm_two(index):
        rows = rows_of(index, TOK_PAD)
        unit, _ = norm_parts(resid[rows, :])
        second[rows, :] = (unit * gains[1:2, :]).astype(low)

    loop(1, norm_two)


def spread_rows(raw, buffer, padded):
    count = raw.shape[0]
    buffer[pl.ds(0, count), :] = raw[...].astype(wide)
    buffer[pl.ds(count, SEQ_PAD - SEQ + 1), :] = jnp.zeros((SEQ_PAD - SEQ + 1, D), wide)
    inside = lax.broadcasted_iota(jnp.int32, (SEQ_PAD, 1), 0) < SEQ
    for image in range(MB * IMG_DEV):
        rows = buffer[pl.ds(image * SEQ, SEQ_PAD), :]
        spot = pl.ds((image % IMG_DEV) * SEQ_PAD, SEQ_PAD)
        padded[image // IMG_DEV, spot, :] = jnp.where(inside, rows, 0.0).astype(low)


def compact_rows(padded, buffer, target):
    for image in range(MB * IMG_DEV):
        spot = pl.ds((image % IMG_DEV) * SEQ_PAD, SEQ_PAD)
        buffer[pl.ds(image * SEQ, SEQ_PAD), :] = padded[image // IMG_DEV, spot, :]
    target[...] = buffer[pl.ds(0, target.shape[0]), :].astype(low)


def place_tokens(route, capacity, named, place, first, count):
    experts = named.shape[0]
    expert_id = lax.broadcasted_iota(jnp.int32, (experts, TOK_PAD), 0)
    is_named = (route[0:1, :] == expert_id) | (route[1:2, :] == expert_id)
    earlier = lax.broadcasted_iota(jnp.int32, (TOK_PAD, TOK_PAD), 0) < lax.broadcasted_iota(
        jnp.int32, (TOK_PAD, TOK_PAD), 1
    )
    ones = jnp.where(is_named, 1.0, 0.0)
    before = dot(ones.astype(low), jnp.where(earlier, 1.0, 0.0).astype(low))
    named[...] = jnp.where(is_named, before, -1.0)
    slot_id = lax.broadcasted_iota(jnp.int32, (capacity, TOK_PAD), 0).astype(wide)

    def one(index):
        hit = slot_id == named[pl.ds(first + index, 1), :]
        place[rows_of(index, capacity), :] = jnp.where(hit, 1.0, 0.0).astype(low)

    loop(count, one)


def split_three(values_in):
    head = values_in.astype(low)
    rest = values_in - head.astype(wide)
    middle = rest.astype(low)
    return [head, middle, (rest - middle.astype(wide)).astype(low)]


def gate_tokens(second, router_t, named, gate):
    logits = dot(router_t[...], second[...], NT)
    is_named = named[...] >= 0.0
    top = jnp.max(jnp.where(is_named, logits, -jnp.inf), axis=0, keepdims=True)
    exp_logits = jnp.where(is_named, jnp.exp(logits - jnp.where(top > -jnp.inf, top, 0.0)), 0.0)
    total = jnp.sum(exp_logits, axis=0, keepdims=True)
    gate[...] = exp_logits / jnp.where(total > 0.0, total, 1.0)


def own_columns(experts, capacity):
    shape = (experts, experts * capacity)
    column = lax.broadcasted_iota(jnp.int32, shape, 1) // capacity
    return column == lax.broadcasted_iota(jnp.int32, shape, 0)


def exact_dot(left, right, dims):
    count = left.shape[0]
    found = dot(jnp.concatenate(split_three(left), axis=0), right, dims)
    return found[0:count] + found[count : 2 * count] + found[2 * count : 3 * count]


def gate_slots(gate, place, capacity, slot_gate):
    experts = gate.shape[0]
    found = exact_dot(gate[...], place[...], NT)
    row = jnp.sum(jnp.where(own_columns(experts, capacity), found, 0.0), axis=0, keepdims=True)
    for expert in range(experts):
        slot_gate[expert, 0:1, 0:capacity] = row[:, expert * capacity : (expert + 1) * capacity]


def backward_scores(
    gains, wout, qkv, probs, resid, grad, attended, proj, scratch, gain_sums, cot, after_norm
):
    def norm_two(index):
        rows = rows_of(index, TOK_PAD)
        unit, inverse = norm_parts(resid[rows, :])
        incoming = grad[rows, :]
        grad_resid = cot[rows, :].astype(wide) + norm_back(
            unit, inverse, gains[1:2, :], incoming
        )
        gain_sums[1] += fold_rows(incoming * unit)
        grad[rows, :] = grad_resid
        attended[rows, :] = grad_resid.astype(low)

    loop(1, norm_two)
    after_norm()

    def through_out(index):
        cols = rows_of(index, COLS)
        scratch[:, cols] = dot(attended[...], wout[cols, :], NT).astype(low)

    loop(D // COLS, through_out)

    def attend(index):
        image, pair = index // PAIRS, index % PAIRS
        rows, cols = rows_of(image, SEQ_PAD), rows_of(pair, 2 * HEAD_DIM)
        query, key, value = qkv[0, rows, cols], qkv[1, rows, cols], qkv[2, rows, cols]
        incoming = scratch[rows, cols]
        shape = (SEQ_PAD, 2 * HEAD_DIM)
        grad_query, grad_key, grad_value = (jnp.zeros(shape, wide) for _ in range(3))
        for half in range(2):
            mask = head_mask(half)
            attn_low = probs[2 * index + half]
            attn = attn_low.astype(wide)
            grad_mixed = jnp.where(mask, incoming, 0.0).astype(low)
            grad_probs = dot(grad_mixed, value, NT)
            grad_value += dot(attn_low, grad_mixed, TN)
            row_dot = jnp.sum(attn * grad_probs, axis=-1, keepdims=True)
            grad_scores = (attn * (grad_probs - row_dot)).astype(low)
            grad_query += dot(grad_scores, jnp.where(mask, key * qk_scale, 0.0).astype(low))
            grad_key += dot(grad_scores, jnp.where(mask, query * qk_scale, 0.0).astype(low), TN)
        proj[0, rows, cols] = grad_query.astype(low)
        proj[1, rows, cols] = grad_key.astype(low)
        proj[2, rows, cols] = grad_value.astype(low)

    loop(IMG_DEV * PAIRS, attend, UNROLL)


def backward_input(tok, gains, wqkv, grad, proj, gain_sums, result):
    def through_qkv(index):
        cols = rows_of(index, COLS)
        total = dot(proj[0], wqkv[0, cols, :], NT)
        total += dot(proj[1], wqkv[1, cols, :], NT)
        result[:, cols] = total + dot(proj[2], wqkv[2, cols, :], NT)

    loop(D // COLS, through_qkv)

    def norm_one(index):
        rows = rows_of(index, TOK_PAD)
        unit, inverse = norm_parts(tok[rows, :].astype(wide))
        incoming = result[rows, :]
        gain_sums[0] += fold_rows(incoming * unit)
        grad[rows, :] += norm_back(unit, inverse, gains[0:1, :], incoming)

    loop(1, norm_one)


ANY = pl.BlockSpec(memory_space=pl.ANY)
VMEM = pl.BlockSpec(memory_space=pltpu.VMEM)
MESH = pl.DeviceIdType.MESH
BLOCK_ROWS = 512
MADE_ROWS = 256
BLOCK_FF = 512
GRAD_FF = 256
REDUCE_ORDER = (3, 0, 1, 2)
KIND_COT, KIND_ROW, KIND_BACK, KIND_MADE, KIND_GATE, KIND_SLOPE = range(6)


def wait_bytes(ref, sem):
    pltpu.make_async_copy(ref, ref, sem).wait()


def local_copy(source, target, sem):
    copy = pltpu.make_async_copy(source, target, sem)
    copy.start()
    return copy


def block_kernel(
    n_dp,
    n_ex,
    capacity,
    tok_in,
    cot_in,
    route_in,
    qkv_in,
    out_in,
    router_in,
    gains_in,
    expert_in,
    expert_out,
    layer_out,
    grad_input,
    share,
    share_small,
    share_in,
    share_out,
    tops_out,
    land,
    half_in,
    half_out,
    spill_probs,
    spill_qkv,
    spill_rows,
    spill_tok,
    spill_cot,
    spill_resid,
    land_qkv,
    land_out,
    hub_rows,
    hub_blocks,
    far_land,
    stage_in,
    stage_out,
    pair_land,
    dp_land,
    part_land,
    route,
    route_far,
    small_own,
    small_land,
    small_t,
    router_low,
    gains,
    second,
    place,
    place_far,
    named,
    named_far,
    gate,
    send,
    hub_buf,
    hub_sums,
    gate_send,
    gate_land,
    slope_send,
    slope_land,
    tops,
    tops_land,
    tops_dp,
    small_sum,
    small_pair,
    small_cut,
    small_dp,
    small_part,
    gain_sums,
    gather_send,
    gather_recv,
    share_send,
    share_sem,
    ex_send,
    ex_recv,
    far_send,
    far_recv,
    full_send,
    full_recv,
    hub_recv,
    sum_send,
    sum_recv,
    route_recv,
    own_near,
    own_far,
    own_hub,
    hub_sem,
    rs_send,
    rs_recv,
    red_send,
    red_recv,
    pair_send,
    pair_recv,
    own_send,
    own_recv,
    chip_send,
    chip_recv,
    core_send,
    core_recv,
    local_sem,
):
    dp, me = lax.axis_index("dp"), lax.axis_index("expert")
    shard = D // n_dp
    slots = n_ex * capacity
    own_rows = rows_of(dp, shard)

    barrier = pltpu.get_barrier_semaphore()

    def greet_ex(step):
        pl.semaphore_signal(
            barrier, inc=1, device_id=(dp, me ^ (step + 1)), device_id_type=MESH
        )

    def greet_dp(step):
        pl.semaphore_signal(
            barrier, inc=1, device_id=(dp ^ (step + 1), me), device_id_type=MESH
        )

    loop(n_ex - 1, greet_ex)
    loop(n_dp - 1, greet_dp)
    pl.semaphore_wait(barrier, n_ex - 1 + n_dp - 1)

    def remote(source, target, send_sem, recv_sem, device):
        pltpu.make_async_remote_copy(
            src_ref=source,
            dst_ref=target,
            send_sem=send_sem,
            recv_sem=recv_sem,
            device_id=device,
            device_id_type=MESH,
        ).start()

    small_own[...] = jnp.zeros(small_own.shape, wide)
    small_own[0:n_ex, 0:shard] = router_in[...].astype(wide)
    small_own[n_ex : n_ex + 2, 0:shard] = gains_in[...].astype(wide)

    def gather_small(step):
        peer = (dp ^ (step + 1), me)
        remote(small_own, small_land.at[dp], gather_send.at[0], gather_recv.at[0], peer)

    core = lax.rem(me, 2)
    partner = (dp, me ^ 1)
    half_shard = shard // 2

    def half_rows_of(owner):
        return pl.ds(pl.multiple_of(owner * shard + core * half_shard, half_shard), half_shard)

    source_rows = rows_of(core, half_shard)

    def gather_qkv(step):
        peer = (dp ^ (step + 1), me)
        remote(
            qkv_in.at[:, source_rows, :],
            land_qkv.at[:, half_rows_of(dp), :],
            gather_send.at[1],
            share_sem.at[0, step],
            peer,
        )

    def gather_out(step):
        peer = (dp ^ (step + 1), me)
        remote(
            out_in.at[source_rows, :],
            land_out.at[half_rows_of(dp), :],
            gather_send.at[2],
            share_sem.at[1, step],
            peer,
        )

    def hand_qkv(step):
        rows = half_rows_of(dp ^ (step + 1))
        part = land_qkv.at[:, rows, :]
        wait_bytes(part, share_sem.at[0, step])
        remote(part, part, share_send.at[0], gather_recv.at[1], partner)

    def hand_out(step):
        rows = half_rows_of(dp ^ (step + 1))
        part = land_out.at[rows, :]
        wait_bytes(part, share_sem.at[1, step])
        remote(part, part, share_send.at[1], gather_recv.at[2], partner)

    loop(n_dp - 1, gather_small)
    loop(n_dp - 1, gather_qkv)
    loop(n_dp - 1, gather_out)
    own_small = local_copy(small_own, small_land.at[dp], local_sem.at[0])

    def load_qkv(target, sem):
        local_copy(qkv_in, target.at[:, own_rows, :], sem)

        def one(step):
            rows = rows_of(dp ^ (step + 1), shard)
            local_copy(land_qkv.at[:, rows, :], target.at[:, rows, :], sem)

        loop(n_dp - 1, one)
        wait_bytes(target, sem)

    def load_out(target, sem):
        local_copy(out_in, target.at[own_rows, :], sem)

        def one(step):
            rows = rows_of(dp ^ (step + 1), shard)
            local_copy(land_out.at[rows, :], target.at[rows, :], sem)

        loop(n_dp - 1, one)
        wait_bytes(target, sem)

    half_ex, quarter_ex = n_ex // 2, n_ex // 4
    half_slots = half_ex * capacity
    side, quarter, rank = me // half_ex, me // quarter_ex, lax.rem(me, quarter_ex)
    first_ex = side * half_ex
    far_ex = (1 - side) * half_ex
    own_index = me - first_ex
    is_hub = (quarter == 1) | (quarter == 2)
    hub = (2 - side) * quarter_ex + rank
    hub_slot = lax.rem(quarter, 2)

    def served(slot):
        return far_ex + slot * quarter_ex + rank

    def block_of(area, index):
        return send.at[area, rows_of(index, capacity), :]

    def wait_blocks(sem, count):
        wait_bytes(send.at[0, pl.ds(0, count * capacity), :], sem)

    def land_block(kind, micro, index):
        return land.at[kind, micro, rows_of(index, capacity), :]

    def near_wait(sems, kind, micro):
        wait_blocks(sems.at[kind, micro], half_ex - 1)

    def far_wait(sems, kind, micro):
        @pl.when(is_hub)
        def _():
            wait_blocks(sems.at[kind, micro], half_ex - 2)

        @pl.when(jnp.logical_not(is_hub))
        def _():
            wait_blocks(sems.at[kind, micro], half_ex)

    def relay_wait(kind, micro):
        @pl.when(is_hub)
        def _():
            wait_blocks(far_send.at[kind, micro], 2 * (half_ex - 1))

    def pack(spot, spot_start, source, area, area_start):
        rows = pl.ds(spot_start, half_slots)
        send[area, pl.ds(area_start, half_slots), :] = dot(spot[rows, :], source[...]).astype(low)

    def spread(area, start, kind, micro, source, send_sem, recv_sem, own_sem):
        def one(step):
            peer = me ^ (step + 1)
            remote(
                block_of(area, start + peer - first_ex),
                land_block(kind, micro, source),
                send_sem,
                recv_sem,
                (dp, peer),
            )

        loop(half_ex - 1, one)
        local_copy(block_of(area, start + own_index), land_block(kind, micro, source), own_sem)

    def scatter_full(kind, micro, source):
        remote(
            source,
            hub_rows.at[kind, micro, hub_slot],
            full_send.at[kind, micro],
            full_recv.at[kind, micro, hub_slot],
            (dp, hub),
        )

    def scatter_near(kind, micro, source):
        area = MB + micro
        pack(place.at[micro], pl.multiple_of(first_ex * capacity, half_slots), source, area, 0)
        spread(
            area,
            0,
            kind,
            micro,
            me,
            ex_send.at[kind, micro],
            ex_recv.at[kind, micro],
            own_near.at[kind, micro],
        )

    def relay(kind, micro):
        @pl.when(is_hub)
        def _():
            if kind == KIND_ROW:
                wait_blocks(far_send.at[KIND_COT, micro], 2 * (half_ex - 1))
                wait_blocks(own_far.at[KIND_COT, micro], 2)

            def fetch(slot):
                wait_bytes(hub_rows.at[kind, micro, slot], full_recv.at[kind, micro, slot])
                local_copy(
                    hub_rows.at[kind, micro, slot],
                    hub_buf.at[slot, pl.ds(0, TOK_PAD), :],
                    hub_sem.at[slot],
                )

            def one(slot):
                rows = hub_buf.at[slot, pl.ds(0, TOK_PAD), :]
                wait_bytes(rows, hub_sem.at[slot])
                pack(
                    place_far.at[micro, slot],
                    0,
                    rows,
                    micro,
                    pl.multiple_of(slot * half_slots, half_slots),
                )
                spread(
                    micro,
                    slot * half_ex,
                    kind,
                    micro,
                    served(slot),
                    far_send.at[kind, micro],
                    far_recv.at[kind, micro],
                    own_far.at[kind, micro],
                )

            loop(2, fetch)
            loop(2, one)

    def gather(kind, micro, area):
        def to_hub(step):
            source = far_ex + step
            slot = lax.rem(source // quarter_ex, 2)
            target = hub_blocks.at[kind - KIND_BACK, micro, slot, rows_of(own_index, capacity), :]
            device = (1 + side) * quarter_ex + lax.rem(source, quarter_ex)

            @pl.when(device == me)
            def _():
                local_copy(block_of(area, source), target, own_hub.at[kind - KIND_BACK, micro, slot])

            @pl.when(device != me)
            def _():
                remote(
                    block_of(area, source),
                    target,
                    far_send.at[kind, micro],
                    hub_recv.at[kind - KIND_BACK, micro, slot],
                    (dp, device),
                )

        def to_near(step):
            peer = me ^ (step + 1)
            remote(
                block_of(area, peer),
                land_block(kind, micro, own_index),
                ex_send.at[kind, micro],
                ex_recv.at[kind, micro],
                (dp, peer),
            )

        loop(half_ex, to_hub)
        loop(half_ex - 1, to_near)
        local_copy(
            block_of(area, me), land_block(kind, micro, own_index), own_near.at[kind, micro]
        )

    def hub_sum(kind, micro):
        index = kind - KIND_BACK

        @pl.when(is_hub)
        def _():
            def fetch(slot):
                if kind == KIND_MADE:
                    wait_bytes(hub_sums.at[micro, slot], sum_send.at[0, micro, slot])
                wait_blocks(hub_recv.at[index, micro, slot], half_ex - 1)
                wait_blocks(own_hub.at[index, micro, slot], 1)
                local_copy(hub_blocks.at[index, micro, slot], hub_buf.at[slot], hub_sem.at[slot])

            def one(slot):
                wait_bytes(hub_buf.at[slot], hub_sem.at[slot])
                hub_sums[micro, slot] = dot(place_far[micro, slot], hub_buf[slot], TN).astype(low)
                remote(
                    hub_sums.at[micro, slot],
                    far_land.at[index, micro],
                    sum_send.at[index, micro, slot],
                    sum_recv.at[index, micro],
                    (dp, served(slot)),
                )

            loop(2, fetch)
            loop(2, one)

    def fetch_gathered(kind, micro, arrived, sem):
        near_wait(ex_recv, kind, micro)
        wait_blocks(own_near.at[kind, micro], 1)
        index = kind - KIND_BACK
        wait_bytes(far_land.at[index, micro], sum_recv.at[index, micro])
        near = arrived.at[pl.ds(0, half_slots), :]
        far = arrived.at[pl.ds(half_slots, TOK_PAD), :]
        local_copy(land.at[kind, micro, pl.ds(0, half_slots), :], near, sem)
        local_copy(far_land.at[index, micro], far, sem)
        wait_bytes(arrived.at[pl.ds(0, half_slots + TOK_PAD), :], sem)

    def gathered(micro, arrived, cols):
        spot = place.at[micro, pl.ds(pl.multiple_of(first_ex * capacity, half_slots), half_slots)]
        near = arrived[pl.ds(0, half_slots), cols]
        far = arrived[pl.ds(half_slots, TOK_PAD), cols]
        return dot(spot[...], near, TN) + far.astype(wide)

    def exchange_small(source, target, kind, micro):
        def one(step):
            peer = me ^ (step + 1)
            remote(
                source.at[micro, peer],
                target.at[micro, me],
                ex_send.at[kind, micro],
                ex_recv.at[kind, micro],
                (dp, peer),
            )

        loop(n_ex - 1, one)
        target[micro, me] = source[micro, me]

    def await_small(sems, ref, kind, micro):
        wait_bytes(ref.at[micro, pl.ds(0, n_ex - 1)], sems.at[kind, micro])

    def forward(wqkv, wout, tok, cot, raw, buffer, probs, qkv, first, mixed, resid, spill_sem):
        def spills(micro):
            tokens = rows_of(micro, TOK_PAD)
            pairs = [
                (probs.at[micro], spill_probs.at[micro]),
                (qkv.at[micro], spill_qkv.at[micro]),
                (first.at[tokens], spill_rows.at[0, tokens]),
                (mixed.at[tokens], spill_rows.at[1, tokens]),
                (resid.at[micro], spill_resid.at[micro]),
            ]
            return [
                pltpu.make_async_copy(source, target, spill_sem.at[micro, index])
                for index, (source, target) in enumerate(pairs)
            ]

        local_copy(cot_in, raw, local_sem.at[3]).wait()
        spread_rows(raw, buffer, cot)
        keep_cot = local_copy(cot, spill_cot, spill_sem.at[MB, 1])
        load = local_copy(tok_in, raw, local_sem.at[3])
        numbers = route_in[...].astype(wide)
        fill = jnp.full((2, SEQ_PAD - SEQ), -1.0, wide)
        for micro in range(MB):
            pieces = []
            for image in range(IMG_DEV):
                start = micro * TOK_MB + image * SEQ
                pieces += [numbers[:, start : start + SEQ], fill]
            route[micro] = jnp.concatenate(pieces, axis=1).astype(jnp.int32)

        remote(
            route, route_far.at[hub_slot], route_recv.at[2], route_recv.at[hub_slot], (dp, hub)
        )
        keep_cot.wait()

        def send_cot(micro):
            scatter_full(KIND_COT, micro, spill_cot.at[micro])
            scatter_near(KIND_COT, micro, cot.at[micro])

        def place_own(micro):
            place_tokens(
                route.at[micro], capacity, named.at[micro], place.at[micro], 0, n_ex
            )

        own_small.wait()
        loop(MB, place_own)
        send_cot(0)

        @pl.when(is_hub)
        def _():
            def one(index):
                micro, slot = index // 2, lax.rem(index, 2)
                place_tokens(
                    route_far.at[slot, micro],
                    capacity,
                    named_far,
                    place_far.at[micro, slot],
                    first_ex,
                    half_ex,
                )

            for slot in range(2):
                wait_bytes(route, route_recv.at[slot])
            loop(2 * MB, one)

        load.wait()
        spread_rows(raw, buffer, tok)
        tops[...] = jnp.full(tops.shape, -jnp.inf, wide)
        wait_bytes(small_land.at[pl.ds(0, n_dp - 1)], gather_recv.at[0])
        for owner in range(n_dp):
            small_t[:, owner * shard : (owner + 1) * shard] = small_land[owner, :, 0:shard]
        router_low[...] = small_t[pl.ds(0, n_ex), :].astype(low)
        gains[...] = small_t[pl.ds(n_ex, 8), :]
        keep_tok = local_copy(tok, spill_tok, spill_sem.at[MB, 0])
        loop(n_dp - 1, hand_qkv)
        wait_bytes(land_qkv.at[:, pl.ds(0, (D - shard) // 2), :], gather_recv.at[1])
        load_qkv(wqkv, local_sem.at[1])

        def out_arrives():
            loop(n_dp - 1, hand_out)

        def out_there():
            wait_bytes(land_out.at[pl.ds(0, (D - shard) // 2), :], gather_recv.at[2])
            load_out(wout, local_sem.at[1])

        def one(micro):
            attention_forward(
                tok.at[micro],
                gains,
                wqkv,
                wout,
                first.at[rows_of(micro, TOK_PAD)],
                qkv.at[micro],
                probs.at[micro],
                mixed.at[rows_of(micro, TOK_PAD)],
                resid.at[micro],
                second.at[rows_of(micro, TOK_PAD)],
                tops,
                lambda: pl.when(micro == 0)(out_arrives),
                lambda: pl.when(micro == 0)(out_there),
            )
            for copy in spills(micro):
                copy.start()
            rows = second.at[rows_of(micro, TOK_PAD)]
            gate_tokens(rows, router_low, named.at[micro], gate.at[micro])
            gate_slots(gate.at[micro], place.at[micro], capacity, gate_send.at[micro])
            exchange_small(gate_send, gate_land, KIND_GATE, micro)
            scatter_full(KIND_ROW, micro, rows)
            near_wait(ex_send, KIND_COT, micro)
            wait_blocks(own_near.at[KIND_COT, micro], 1)
            scatter_near(KIND_ROW, micro, rows)

            @pl.when(micro == 0)
            def _():
                send_cot(1)
                relay(KIND_COT, 0)


        loop(MB, one)

        def spread_top(step):
            peer = me ^ (step + 1)
            remote(tops, tops_land.at[me], red_send.at[0], red_recv.at[0], (dp, peer))

        loop(n_ex - 1, spread_top)
        tops_land[me] = tops[...]
        for micro in range(MB):
            for copy in spills(micro):
                copy.wait()
        keep_tok.wait()

    pl.run_scoped(
        forward,
        pltpu.VMEM((3, D, D), low),
        pltpu.VMEM((D, D), low),
        pltpu.VMEM((MB, TOK_PAD, D), low),
        pltpu.VMEM((MB, TOK_PAD, D), low),
        pltpu.VMEM((MB * TOK_MB, D), low),
        pltpu.VMEM((MB * TOK_MB + SEQ_PAD - SEQ + 1, D), wide),
        pltpu.VMEM((MB, IMG_DEV * HEADS, SEQ_PAD, SEQ_PAD), low),
        pltpu.VMEM((MB, 3, TOK_PAD, D), low),
        pltpu.VMEM((MB * TOK_PAD, D), low),
        pltpu.VMEM((MB * TOK_PAD, D), low),
        pltpu.VMEM((MB, TOK_PAD, D), wide),
        pltpu.SemaphoreType.DMA((MB + 1, 5)),
    )

    def experts(
        w_in,
        w_out,
        rows_in,
        cot,
        grad_rows,
        rows_t,
        grad_t,
        hidden,
        grad_pre,
        made,
        first_grads,
        sems,
    ):
        eye = lax.broadcasted_iota(jnp.int32, (capacity, capacity), 0) == lax.broadcasted_iota(
            jnp.int32, (capacity, capacity), 1
        )

        def gate_column(micro, source):
            row = gate_land[micro, source, 0:1, 0:capacity]
            return jnp.sum(jnp.where(eye, row, 0.0), axis=1, keepdims=True)

        loads = [
            local_copy(expert_in, w_in, local_sem.at[4]),
            local_copy(expert_out, w_out, local_sem.at[5]),
        ]
        relay(KIND_ROW, 0)
        for copy in loads:
            copy.wait()

        def one(micro):
            pl.when(micro > 0)(lambda: relay(KIND_ROW, 1))
            near_wait(ex_recv, KIND_COT, micro)
            far_wait(far_recv, KIND_COT, micro)
            await_small(ex_recv, gate_land, KIND_GATE, micro)
            near_wait(ex_recv, KIND_ROW, micro)
            far_wait(far_recv, KIND_ROW, micro)
            wait_blocks(own_near.at[KIND_ROW, micro], 1)

            @pl.when(is_hub)
            def _():
                wait_blocks(own_far.at[KIND_ROW, micro], 2)

            load_rows = local_copy(land.at[KIND_ROW, micro], rows_in, sems.at[0])
            load_cot = local_copy(land.at[KIND_COT, micro], cot, sems.at[1])
            load_rows.wait()
            load_cot.wait()

            def scale(source):
                rows = rows_of(source, capacity)
                wide_cot = cot[rows, :].astype(wide)
                grad_rows[rows, :] = (wide_cot * gate_column(micro, source)).astype(low)

            loop(n_ex, scale)

            def turn(index):
                rows = rows_of(index, 128)
                cols = pl.ds(pl.multiple_of(index * 128, 128), 128)
                rows_t[:, cols] = rows_in[rows, :].T
                grad_t[:, cols] = grad_rows[rows, :].T

            loop(slots // 128, turn)

            def through(index):
                cols = rows_of(index // (slots // BLOCK_ROWS), BLOCK_FF)
                rows = rows_of(index % (slots // BLOCK_ROWS), BLOCK_ROWS)
                value, slope = gelu_both(dot(rows_in[rows, :], w_in[:, cols]))
                hidden[rows, cols] = value.astype(low)
                grad_hidden = dot(grad_rows[rows, :], w_out[cols, :], NT)
                grad_pre[rows, cols] = (grad_hidden * slope).astype(low)

            loop((FF // BLOCK_FF) * (slots // BLOCK_ROWS), through, 2)

            relay_wait(KIND_ROW, micro)

            def back(index):
                rows = rows_of(index, BLOCK_ROWS)
                send[micro, rows, :] = dot(grad_pre[rows, :], w_in[...], NT).astype(low)

            loop(slots // BLOCK_ROWS, back)
            gather(KIND_BACK, micro, micro)
            near_wait(ex_send, KIND_ROW, micro)

            def forth(index):
                rows = rows_of(index, MADE_ROWS)
                made[...] = dot(hidden[rows, :], w_out[...])
                count = MADE_ROWS // capacity

                def finish(part):
                    source = index * count + part
                    own = rows_of(source, capacity)
                    values = made[rows_of(part, capacity), :]
                    column = jnp.sum(values * cot[own, :].astype(wide), axis=1, keepdims=True)
                    slope_send[micro, source, 0:1, 0:capacity] = jnp.sum(
                        jnp.where(eye, column, 0.0), axis=0, keepdims=True
                    )
                    send[MB + micro, own, :] = (values * gate_column(micro, source)).astype(low)

                loop(count, finish)

            loop(slots // MADE_ROWS, forth)
            exchange_small(slope_send, slope_land, KIND_SLOPE, micro)

            @pl.when(micro == 0)
            def _():
                relay(KIND_COT, 1)
                first_grads()

        loop(MB, one)
        hub_sum(KIND_BACK, 0)
        loop(MB, lambda micro: gather(KIND_MADE, micro, MB + micro))

        wait_bytes(tops_land.at[pl.ds(0, n_ex - 1)], red_recv.at[0])
        wait_bytes(tops_land.at[pl.ds(0, n_ex - 1)], red_send.at[0])
        tops[...] = jnp.max(tops_land[...], axis=0)

    def expert_phase(
        w_in,
        w_out,
        rows_in,
        cot,
        grad_rows,
        rows_t,
        grad_t,
        hidden,
        grad_pre,
        made,
        kept_in,
        kept_out,
        block_in,
        block_out,
        load_sems,
        store_sems,
        sems,
    ):
        blocks = FF // GRAD_FF

        def stores(block, slot, target_in, target_out):
            cols = rows_of(block, GRAD_FF)
            return (
                pltpu.make_async_copy(
                    block_in.at[slot], target_in.at[:, cols], store_sems.at[0, slot]
                ),
                pltpu.make_async_copy(
                    block_out.at[slot], target_out.at[:, cols], store_sems.at[1, slot]
                ),
            )

        def own_store(block, slot):
            cols = rows_of(block, GRAD_FF)
            return pltpu.make_async_copy(
                block_in.at[slot, own_rows, :], share_in.at[dp, :, cols], store_sems.at[2, slot]
            )

        def first_grads():
            def one(block):
                slot = lax.rem(block, 2)

                @pl.when(block > 1)
                def _():
                    for copy in stores(block - 2, slot, half_in, half_out):
                        copy.wait()

                cols = rows_of(block, GRAD_FF)
                block_in[slot] = dot(rows_t[...], grad_pre[:, cols]).astype(low)
                block_out[slot] = dot(grad_t[...], hidden[:, cols]).astype(low)
                for copy in stores(block, slot, half_in, half_out):
                    copy.start()

            loop(blocks, one)
            for block in (blocks - 2, blocks - 1):
                for copy in stores(block, block % 2, half_in, half_out):
                    copy.wait()

        def second_grads():
            def fetch(block, slot):
                cols = rows_of(block, GRAD_FF)
                local_copy(half_in.at[:, cols], kept_in.at[slot], load_sems.at[0, slot])
                local_copy(half_out.at[:, cols], kept_out.at[slot], load_sems.at[1, slot])

            def ship(block, slot):
                for copy in stores(block, slot, stage_in, stage_out):
                    copy.wait()
                own_store(block, slot).wait()
                cols = rows_of(block, GRAD_FF)

                def one(step):
                    peer = dp ^ (step + 1)
                    remote(
                        stage_in.at[rows_of(peer, shard), cols],
                        share_in.at[dp, :, cols],
                        rs_send.at[0],
                        rs_recv.at[0],
                        (peer, me),
                    )

                loop(n_dp - 1, one)

            fetch(0, 0)

            def one(block):
                slot = lax.rem(block, 2)

                @pl.when(block + 1 < blocks)
                def _():
                    fetch(block + 1, 1 - slot)

                wait_bytes(kept_in.at[slot], load_sems.at[0, slot])
                wait_bytes(kept_out.at[slot], load_sems.at[1, slot])
                cols = rows_of(block, GRAD_FF)
                value_in = dot(rows_t[...], grad_pre[:, cols]) + kept_in[slot].astype(wide)
                block_in[slot] = value_in.astype(low)
                value_out = dot(grad_t[...], hidden[:, cols]) + kept_out[slot].astype(wide)
                block_out[slot] = value_out.astype(low)
                for copy in stores(block, slot, stage_in, stage_out):
                    copy.start()
                own_store(block, slot).start()

                @pl.when(block > 0)
                def _():
                    ship(block - 1, 1 - slot)

            loop(blocks, one)
            ship(blocks - 1, (blocks - 1) % 2)

        experts(
            w_in,
            w_out,
            rows_in,
            cot,
            grad_rows,
            rows_t,
            grad_t,
            hidden,
            grad_pre,
            made,
            first_grads,
            sems,
        )
        second_grads()
        hub_sum(KIND_BACK, 1)

    pl.run_scoped(
        expert_phase,
        pltpu.VMEM((D, FF), low),
        pltpu.VMEM((FF, D), low),
        pltpu.VMEM((slots, D), low),
        pltpu.VMEM((slots, D), low),
        pltpu.VMEM((slots, D), low),
        pltpu.VMEM((D, slots), low),
        pltpu.VMEM((D, slots), low),
        pltpu.VMEM((slots, FF), low),
        pltpu.VMEM((slots, FF), low),
        pltpu.VMEM((MADE_ROWS, D), wide),
        pltpu.VMEM((2, D, GRAD_FF), low),
        pltpu.VMEM((2, D, GRAD_FF), low),
        pltpu.VMEM((2, D, GRAD_FF), low),
        pltpu.VMEM((2, D, GRAD_FF), low),
        pltpu.SemaphoreType.DMA((2, 2)),
        pltpu.SemaphoreType.DMA((3, 2)),
        pltpu.SemaphoreType.DMA((4,)),
    )

    width = FF // n_dp

    def ship_out(step, rows=pl.ds(0, D)):
        peer = dp ^ (step + 1)
        remote(
            stage_out.at[rows, rows_of(peer, width)],
            share_out.at[dp, rows, :],
            rs_send.at[1],
            rs_recv.at[1],
            (peer, me),
        )

    loop(2, ship_out)

    def spread_tops(step):
        peer = dp ^ (step + 1)
        remote(tops, tops_dp.at[dp], red_send.at[1], red_recv.at[1], (peer, me))

    loop(n_dp - 1, spread_tops)
    tops_dp[dp] = tops[...]

    chips = parts = n_ex // 2
    part_rows = part_size(n_dp, n_ex)
    z = me // 2

    def backward(
        wqkv,
        wout,
        resid,
        cot,
        probs,
        qkv,
        first,
        mixed,
        arrived,
        grad,
        attended,
        proj,
        result,
        grads,
        pairs,
        total_rows,
        grad_low,
        summed,
        part_own,
        buffer,
        compact,
        sems,
    ):
        first_loads = [
            local_copy(source, target, sems.at[index])
            for index, (source, target) in enumerate(
                [
                    (spill_rows.at[0], first),
                    (spill_rows.at[1], mixed),
                    (spill_resid, resid),
                ]
            )
        ]
        kept_out = arrived.at[pl.ds(0, D), pl.ds(0, width)]
        local_copy(stage_out.at[:, rows_of(dp, width)], kept_out, sems.at[5]).wait()
        local_copy(kept_out, share_out.at[dp], sems.at[5]).wait()
        gain_sums[...] = jnp.zeros(gain_sums.shape, wide)
        small_sum[...] = jnp.zeros(small_sum.shape, wide)
        for copy in first_loads:
            copy.wait()
        load_qkv(wqkv, sems.at[4])
        load_out(wout, sems.at[4])

        def own_half(which):
            return pl.ds(pl.multiple_of(which * half_shard, half_shard), half_shard)

        def to_partner(part):
            remote(
                grads.at[part, :, own_half(1 - core), :],
                pair_land.at[part],
                pair_send.at[part],
                pair_recv.at[part],
                partner,
            )

        def to_owners(part):
            wait_bytes(pair_land.at[part], pair_recv.at[part])
            local_copy(pair_land.at[part], pairs.at[part], sems.at[5]).wait()

            def add_pair(owner):
                mine = grads[part, owner, own_half(core), :].astype(wide)
                pairs[part, owner] = (mine + pairs[part, owner].astype(wide)).astype(low)

            loop(n_dp, add_pair)

            def one(step):
                peer = dp ^ (step + 1)
                remote(
                    pairs.at[part, peer],
                    dp_land.at[dp, own_half(REDUCE_ORDER.index(part)), :],
                    own_send.at[part],
                    own_recv.at[part],
                    (peer, me),
                )

            loop(n_dp - 1, one)

        def grad_block(part, left, right):
            def one(block):
                cols = rows_of(block, COLS)
                value = dot(left[...], right[:, cols], TN).astype(low)
                for owner in range(n_dp):
                    grads[part, owner, :, cols] = value[owner * shard : (owner + 1) * shard, :]

            loop(D // COLS, one)
            to_partner(part)

        def one(micro):
            tokens = rows_of(micro, TOK_PAD)
            loads = [
                local_copy(spill_probs.at[micro], probs, sems.at[0]),
                local_copy(spill_qkv.at[micro], qkv, sems.at[1]),
                local_copy(spill_cot.at[micro], cot, sems.at[2]),
            ]
            await_small(ex_recv, slope_land, KIND_SLOPE, micro)
            fetch_gathered(KIND_BACK, micro, arrived, sems.at[3])
            row = jnp.concatenate(
                [slope_land[micro, expert, 0:1, 0:capacity] for expert in range(n_ex)], axis=1
            )
            blocks = jnp.where(own_columns(n_ex, capacity), row, 0.0)
            slope = exact_dot(blocks, place[micro], NN)
            gates = gate[micro]
            grad_logits = gates * (slope - jnp.sum(gates * slope, axis=0, keepdims=True))
            grad_logits = grad_logits.astype(low)
            small_sum[pl.ds(0, n_ex), :] += dot(grad_logits, second[tokens, :])
            for block in range(D // COLS):
                cols = pl.ds(block * COLS, COLS)
                grad[micro, :, cols] = gathered(micro, arrived, cols) + dot(
                    grad_logits, router_low[:, cols], TN
                )
            for load in loads:
                load.wait()
            backward_scores(
                gains,
                wout,
                qkv,
                probs,
                resid.at[micro],
                grad.at[micro],
                attended.at[tokens],
                proj.at[:, tokens, :],
                arrived.at[pl.ds(0, TOK_PAD), :],
                gain_sums,
                cot,
                lambda: pl.when(micro == MB - 1)(lambda: grad_block(3, mixed, attended)),
            )

            pl.when(micro == 0)(lambda: hub_sum(KIND_MADE, 0))


        loop(MB, one)
        half_rows = pl.ds(0, shard)

        def chip(index):
            return (dp, 2 * index + core)

        mine = rows_of(z, part_rows)

        def to_chips(group):
            for slot in range(2):
                position = 2 * group + slot
                part = REDUCE_ORDER[position]
                wait_bytes(
                    dp_land.at[pl.ds(0, n_dp - 1), own_half(position), :], own_recv.at[part]
                )
                total_rows[own_half(slot), :] = pairs[part, dp].astype(wide)

            def place_for(step):
                return qkv.at[lax.rem(step, 3), rows_of(step // 3, shard), :]

            def load(step):
                peer = dp ^ (step + 1)
                local_copy(dp_land.at[peer, rows_of(group, shard), :], place_for(step), sems.at[0])

            loop(n_dp - 1, load)
            wait_bytes(dp_land.at[pl.ds(0, n_dp - 1), half_rows, :], sems.at[0])

            def add(step):
                total_rows[half_rows, :] += place_for(step)[...].astype(wide)

            loop(n_dp - 1, add)
            total = parts * part_rows
            if total > shard:
                grad_low[group, pl.ds(shard, total - shard), :] = jnp.zeros(
                    (total - shard, D), low
                )
            grad_low[group, half_rows, :] = total_rows[half_rows, :].astype(low)

            def one(step):
                peer = z ^ (step + 1)
                remote(
                    grad_low.at[group, rows_of(peer, part_rows), :],
                    part_land.at[group, z],
                    chip_send.at[0, group],
                    chip_recv.at[0, group],
                    chip(peer),
                )

            loop(parts - 1, one)

        def to_all_chips(group):
            wait_bytes(part_land.at[group, pl.ds(0, parts - 1)], chip_recv.at[0, group])

            def load(step):
                peer = z ^ (step + 1)
                local_copy(part_land.at[group, peer], part_own.at[step], sems.at[0])

            loop(parts - 1, load)
            part_total = total_rows.at[pl.ds(0, part_rows), :]
            part_total[...] = grad_low[group, mine, :].astype(wide)
            wait_bytes(part_own, sems.at[0])

            def add(step):
                part_total[...] += part_own[step].astype(wide)

            loop(parts - 1, add)
            summed[group] = part_total[...].astype(low)

            def one(step):
                peer = z ^ (step + 1)
                remote(
                    summed.at[group],
                    share.at[core, group, mine, :],
                    chip_send.at[1, group],
                    chip_recv.at[1, group],
                    chip(peer),
                )

            loop(parts - 1, one)
            local_copy(summed.at[group], share.at[core, group, mine, :], sems.at[0]).wait()

        def to_core(group):
            wait_bytes(
                share.at[0, group, pl.ds(0, (parts - 1) * part_rows), :], chip_recv.at[1, group]
            )
            half = share.at[core, group, half_rows, :]
            remote(half, half, core_send.at[group], core_recv.at[group], partner)

        hub_sum(KIND_MADE, 1)
        grad_block(0, first, proj.at[0])
        to_owners(3)
        grad_block(1, first, proj.at[1])
        to_owners(0)
        grad_block(2, first, proj.at[2])
        to_owners(1)
        to_owners(2)
        loop(n_dp - 3, lambda step: ship_out(step + 2, pl.ds(0, D // 2)))
        to_chips(0)

        def finish(micro):
            local_copy(spill_tok.at[micro], cot, sems.at[2]).wait()
            backward_input(
                cot,
                gains,
                wqkv,
                grad.at[micro],
                proj.at[:, rows_of(micro, TOK_PAD), :],
                gain_sums,
                result,
            )

        finish(0)
        to_all_chips(0)
        finish(1)
        small_sum[n_ex : n_ex + 1, :] = jnp.sum(gain_sums[0], axis=0, keepdims=True)
        small_sum[n_ex + 1 : n_ex + 2, :] = jnp.sum(gain_sums[1], axis=0, keepdims=True)
        remote(small_sum, small_pair, red_send.at[3], red_recv.at[3], partner)
        compact_rows(grad, buffer, compact)
        store = local_copy(compact, grad_input, sems.at[4])
        wait_bytes(small_pair, red_recv.at[3])
        both = small_sum[...] + small_pair[...]
        small_cut[...] = jnp.zeros(small_cut.shape, wide)
        for owner in range(n_dp):
            small_cut[owner, :, 0:shard] = both[:, owner * shard : (owner + 1) * shard]

        def small_to_owner(step):
            peer = dp ^ (step + 1)
            remote(
                small_cut.at[peer], small_dp.at[dp], red_send.at[5], red_recv.at[5], (peer, me)
            )

        loop(n_dp - 1, small_to_owner)
        loop(n_dp - 3, lambda step: ship_out(step + 2, pl.ds(D // 2, D // 2)))
        small_dp[dp] = small_cut[dp]
        to_chips(1)
        to_core(0)
        wait_bytes(small_dp.at[pl.ds(0, n_dp - 1)], red_recv.at[5])
        small_part[me] = jnp.sum(small_dp[...], axis=0)

        def to_chip(step):
            remote(
                small_part.at[me],
                small_part.at[me],
                red_send.at[7],
                red_recv.at[7],
                chip(z ^ (step + 1)),
            )

        loop(parts - 1, to_chip)
        to_all_chips(1)

        def combine(micro):
            fetch_gathered(KIND_MADE, micro, arrived, sems.at[3])
            for block in range(D // COLS):
                cols = pl.ds(block * COLS, COLS)
                grad[micro, :, cols] = resid[micro, :, cols] + gathered(micro, arrived, cols)

        combine(0)
        to_core(1)
        combine(1)
        store.wait()
        compact_rows(grad, buffer, compact)
        store = local_copy(compact, layer_out, sems.at[4])
        wait_bytes(small_part.at[pl.ds(0, parts - 1)], red_recv.at[7])
        chosen = small_part[core]
        for index in range(1, chips):
            chosen += small_part[2 * index + core]
        share_small[...] = chosen
        wait_bytes(tops_dp.at[pl.ds(0, n_dp - 1)], red_recv.at[1])
        tops_out[...] = jnp.max(tops_dp[...], axis=0)
        for group in range(2):
            wait_bytes(share.at[0, group, half_rows, :], core_recv.at[group])
        store.wait()

        for part in range(4):
            wait_bytes(pair_land.at[part], pair_send.at[part])
            wait_bytes(dp_land.at[pl.ds(0, n_dp - 1), own_half(part), :], own_send.at[part])
        for group in range(2):
            for step in range(2):
                wait_bytes(
                    grad_low.at[0, pl.ds(0, (parts - 1) * part_rows), :],
                    chip_send.at[step, group],
                )

    pl.run_scoped(
        backward,
        pltpu.VMEM((3, D, D), low),
        pltpu.VMEM((D, D), low),
        pltpu.VMEM((MB, TOK_PAD, D), wide),
        pltpu.VMEM((TOK_PAD, D), low),
        pltpu.VMEM((IMG_DEV * HEADS, SEQ_PAD, SEQ_PAD), low),
        pltpu.VMEM((3, TOK_PAD, D), low),
        pltpu.VMEM((MB * TOK_PAD, D), low),
        pltpu.VMEM((MB * TOK_PAD, D), low),
        pltpu.VMEM((slots, D), low),
        pltpu.VMEM((MB, TOK_PAD, D), wide),
        pltpu.VMEM((MB * TOK_PAD, D), low),
        pltpu.VMEM((3, MB * TOK_PAD, D), low),
        pltpu.VMEM((TOK_PAD, D), wide),
        pltpu.VMEM((4, n_dp, shard, D), low),
        pltpu.VMEM((4, n_dp, half_shard, D), low),
        pltpu.VMEM((max(shard, part_rows), D), wide),
        pltpu.VMEM((2, parts * part_rows, D), low),
        pltpu.VMEM((2, part_rows, D), low),
        pltpu.VMEM((parts - 1, part_rows, D), low),
        pltpu.VMEM((MB * TOK_MB + SEQ_PAD - SEQ + 1, D), wide),
        pltpu.VMEM((MB * TOK_MB, D), low),
        pltpu.SemaphoreType.DMA((6,)),
    )

    wait_bytes(share_in.at[pl.ds(0, n_dp - 1)], rs_recv.at[0])
    wait_bytes(share_out.at[pl.ds(0, n_dp - 1)], rs_recv.at[1])
    wait_bytes(share_in.at[pl.ds(0, n_dp - 1)], rs_send.at[0])
    wait_bytes(share_out.at[pl.ds(0, n_dp - 1)], rs_send.at[1])
    wait_bytes(small_land.at[pl.ds(0, n_dp - 1)], gather_send.at[0])
    wait_bytes(small_pair, red_send.at[3])
    others_half = pl.ds(0, (D - shard) // 2)
    for sems in (gather_send.at[1], share_send.at[0]):
        wait_bytes(land_qkv.at[:, others_half, :], sems)
    for sems in (gather_send.at[2], share_send.at[1]):
        wait_bytes(land_out.at[others_half, :], sems)
    wait_bytes(route, route_recv.at[2])
    for micro in range(MB):
        for kind in (KIND_COT, KIND_ROW):
            wait_bytes(spill_cot.at[micro], full_send.at[kind, micro])
        for kind in (KIND_BACK, KIND_MADE):
            near_wait(ex_send, kind, micro)
            far_wait(far_send, kind, micro)
        await_small(ex_send, gate_land, KIND_GATE, micro)
        await_small(ex_send, slope_land, KIND_SLOPE, micro)
    wait_bytes(tops_dp.at[pl.ds(0, n_dp - 1)], red_send.at[1])

    @pl.when(is_hub)
    def _():
        for micro in range(MB):
            for slot in range(2):
                wait_bytes(hub_sums.at[micro, slot], sum_send.at[1, micro, slot])

    wait_bytes(small_dp.at[pl.ds(0, n_dp - 1)], red_send.at[5])
    wait_bytes(small_part.at[pl.ds(0, parts - 1)], red_send.at[7])
    for group in range(2):
        wait_bytes(share.at[0, group, pl.ds(0, shard), :], core_send.at[group])


def part_size(n_dp, n_ex):
    shard, parts = D // n_dp, n_ex // 2
    return -(-shard // (parts * 16)) * 16


def run_block(n_dp, n_ex, capacity, operands):
    shard, slots = D // n_dp, n_ex * capacity
    parts, part_rows = n_ex // 2, part_size(n_dp, n_ex)
    total = parts * part_rows
    lanes = -(-shard // 128) * 128
    outs = [
        ((MB * TOK_MB, D), low),
        ((MB * TOK_MB, D), low),
        ((2, 2, total, D), low),
        ((n_ex + 8, lanes), wide),
        ((n_dp, shard, FF), low),
        ((n_dp, D, FF // n_dp), low),
        ((16, 128), wide),
        ((4, MB, slots, D), low),
        ((D, FF), low),
        ((D, FF), low),
        ((MB, IMG_DEV * HEADS, SEQ_PAD, SEQ_PAD), low),
        ((MB, 3, TOK_PAD, D), low),
        ((2, MB * TOK_PAD, D), low),
        ((MB, TOK_PAD, D), low),
        ((MB, TOK_PAD, D), low),
        ((MB, TOK_PAD, D), wide),
        ((3, D, D), low),
        ((D, D), low),
        ((2, MB, 2, TOK_PAD, D), low),
        ((2, MB, 2, slots // 2, D), low),
        ((2, MB, TOK_PAD, D), low),
        ((D, FF), low),
        ((D, FF), low),
        ((4, n_dp, shard // 2, D), low),
        ((n_dp, 2 * shard, D), low),
        ((2, parts, part_rows, D), low),
    ]
    in_vmem = (3, 6)
    return pl.pallas_call(
        functools.partial(block_kernel, n_dp, n_ex, capacity),
        out_shape=[jax.ShapeDtypeStruct(*one) for one in outs],
        in_specs=[ANY, ANY, VMEM, ANY, ANY, VMEM, VMEM, ANY, ANY],
        out_specs=[VMEM if index in in_vmem else ANY for index in range(len(outs))],
        scratch_shapes=[
            pltpu.VMEM((MB, 2, TOK_PAD), jnp.int32),
            pltpu.VMEM((2, MB, 2, TOK_PAD), jnp.int32),
            pltpu.VMEM((n_ex + 8, lanes), wide),
            pltpu.VMEM((n_dp, n_ex + 8, lanes), wide),
            pltpu.VMEM((n_ex + 8, D), wide),
            pltpu.VMEM((n_ex, D), low),
            pltpu.VMEM((8, D), wide),
            pltpu.VMEM((MB * TOK_PAD, D), low),
            pltpu.VMEM((MB, slots, TOK_PAD), low),
            pltpu.VMEM((MB, 2, slots // 2, TOK_PAD), low),
            pltpu.VMEM((MB, n_ex, TOK_PAD), wide),
            pltpu.VMEM((n_ex, TOK_PAD), wide),
            pltpu.VMEM((MB, n_ex, TOK_PAD), wide),
            pltpu.VMEM((2 * MB, slots, D), low),
            pltpu.VMEM((2, slots // 2, D), low),
            pltpu.VMEM((MB, 2, TOK_PAD, D), low),
            pltpu.VMEM((MB, n_ex, 8, 128), wide),
            pltpu.VMEM((MB, n_ex, 8, 128), wide),
            pltpu.VMEM((MB, n_ex, 8, 128), wide),
            pltpu.VMEM((MB, n_ex, 8, 128), wide),
            pltpu.VMEM((16, 128), wide),
            pltpu.VMEM((n_ex, 16, 128), wide),
            pltpu.VMEM((n_dp, 16, 128), wide),
            pltpu.VMEM((n_ex + 8, D), wide),
            pltpu.VMEM((n_ex + 8, D), wide),
            pltpu.VMEM((n_dp, n_ex + 8, lanes), wide),
            pltpu.VMEM((n_dp, n_ex + 8, lanes), wide),
            pltpu.VMEM((n_ex, n_ex + 8, lanes), wide),
            pltpu.VMEM((2, 8, D), wide),
            pltpu.SemaphoreType.DMA((3,)),
            pltpu.SemaphoreType.DMA((3,)),
            pltpu.SemaphoreType.DMA((2,)),
            pltpu.SemaphoreType.DMA((2, n_dp - 1)),
            pltpu.SemaphoreType.DMA((6, MB)),
            pltpu.SemaphoreType.DMA((6, MB)),
            pltpu.SemaphoreType.DMA((4, MB)),
            pltpu.SemaphoreType.DMA((4, MB)),
            pltpu.SemaphoreType.DMA((2, MB)),
            pltpu.SemaphoreType.DMA((2, MB, 2)),
            pltpu.SemaphoreType.DMA((2, MB, 2)),
            pltpu.SemaphoreType.DMA((2, MB, 2)),
            pltpu.SemaphoreType.DMA((2, MB)),
            pltpu.SemaphoreType.DMA((3,)),
            pltpu.SemaphoreType.DMA((4, MB)),
            pltpu.SemaphoreType.DMA((2, MB)),
            pltpu.SemaphoreType.DMA((2, MB, 2)),
            pltpu.SemaphoreType.DMA((2,)),
            pltpu.SemaphoreType.DMA((2,)),
            pltpu.SemaphoreType.DMA((2,)),
            pltpu.SemaphoreType.DMA((10,)),
            pltpu.SemaphoreType.DMA((10,)),
            pltpu.SemaphoreType.DMA((4,)),
            pltpu.SemaphoreType.DMA((4,)),
            pltpu.SemaphoreType.DMA((4,)),
            pltpu.SemaphoreType.DMA((4,)),
            pltpu.SemaphoreType.DMA((2, 2)),
            pltpu.SemaphoreType.DMA((2, 2)),
            pltpu.SemaphoreType.DMA((2,)),
            pltpu.SemaphoreType.DMA((2,)),
            pltpu.SemaphoreType.DMA((6,)),
        ],
        compiler_params=pltpu.CompilerParams(
            collective_id=0, has_side_effects=True, vmem_limit_bytes=61 * 2**20
        ),
        name="encoder_block",
    )(*operands)


def per_device(
    tokens,
    attn_qkv,
    attn_out,
    router,
    norm_gains,
    expert_in,
    expert_out,
    routes,
    clip_limit,
    cotangent,
):
    n_dp, n_ex = lax.axis_size("dp"), lax.axis_size("expert")
    capacity = max(8, (TOK_MB * 10 // (4 * n_ex) + 7) // 8 * 8)
    shard = D // n_dp
    results = run_block(
        n_dp,
        n_ex,
        capacity,
        (
            tokens,
            cotangent,
            routes.T,
            attn_qkv,
            attn_out,
            router.T,
            norm_gains,
            expert_in[0],
            expert_out[0],
        ),
    )
    layer_out, grad_input, share, share_small, share_in, share_out, tops = results[:7]
    share = share[:, :, :shard].reshape(2, 4, shard // 2, D).astype(wide)
    share = jnp.swapaxes(share, 0, 1).reshape(4, shard, D)
    head_max = tops[:HEADS, 0]
    factor = clip_limit / jnp.maximum(head_max, clip_limit)
    root_scale = jnp.repeat(jnp.sqrt(factor), HEAD_DIM)
    clipped_qk = attn_qkv[:2].astype(wide) * root_scale[None, None, :]
    return (
        layer_out,
        grad_input,
        share[1:],
        share[0],
        share_small[:n_ex, :shard].T,
        share_small[n_ex : n_ex + 2, :shard],
        jnp.sum(share_in.astype(wide), axis=0)[None],
        jnp.sum(share_out.astype(wide), axis=0).T[None],
        head_max,
        clipped_qk,
    )


def solution(mesh):
    placed = (
        P(("dp", "expert"), None),
        P(None, "dp", None),
        P("dp", None),
        P("dp", None),
        P(None, "dp"),
        P("expert", None, None),
        P("expert", None, None),
        P(("dp", "expert"), None),
        P(),
        P(("dp", "expert"), None),
    )
    return jax.shard_map(
        per_device,
        mesh=mesh,
        in_specs=placed,
        out_specs=(
            P(("dp", "expert"), None),
            P(("dp", "expert"), None),
            P(None, "dp", None),
            P("dp", None),
            P("dp", None),
            P(None, "dp"),
            P("expert", "dp", None),
            P("expert", "dp", None),
            P(),
            P(None, "dp", None),
        ),
        check_vma=False,
    )
```
